512 devices in a mesh: section: 4 (over x), expert: 128 (over z, y, core).
Axes of the slice: x: 4, y: 4, z: 16, core: 2. Of those that a mesh axis runs over, the one named last changes fastest.
Arguments:
- hidden_rows: bfloat16 [4, 1024, 3584], P('section', 'expert'), may hold values from -6 to 6
- expert_ids: int32 [4, 1024, 2], P('section', 'expert'), may hold values from 0 to 7, all different within a row; in each aligned block of 8 rows (0 to 7, 8 to 15, ..., all dimensions but the last counted through in order) at most 2 rows name the same one
- gate_weights: float32 [4, 1024, 2], P('section', 'expert'), may hold values from 0.2 to 2
- w_gate: bfloat16 [4, 3584, 16384], P('section', None, 'expert'), may hold values from -0.09375 to 0.09375
- w_up: bfloat16 [4, 3584, 16384], P('section', None, 'expert'), may hold values from -0.09375 to 0.09375
- w_down: bfloat16 [4, 16384, 3584], P('section', 'expert'), may hold values from -0.125 to 0.125
- query_latent: bfloat16 [4, 1024, 32, 512], P('section', 'expert')
- query_rope: bfloat16 [4, 1024, 2048], P('section', 'expert')
- cache_latent: bfloat16 [4, 8192, 512], P('section', 'expert'), may hold values from -4 to 4
- cache_rope: bfloat16 [4, 8192, 64], P('section', 'expert'), may hold values from -4 to 4
- offsets: int32 [4], P('section'), may hold values from 0 to 7168
Outputs:
- passed: bfloat16 [4, 1024, 3584], P('section', 'expert')
- attended: bfloat16 [4, 1024, 32, 512], P('section', 'expert')
The draws below stay inside these ranges and needn't reach their ends.
Inputs may be any that keep to these rules, and one draw needn't show every extreme that they name: `expert_ids`: each row names 2 different experts. In every aligned block of 8 rows (the tokens of one device), no expert is named by more than 2 rows, a bound that some block reaches.
All inputs are finite; a program needn't handle non-finite values.
Results may differ from the reference program's by a relative error of at most 0.014.
Values may be sent and summed in bfloat16 or wider, within the bound.
A program may use at most 64 MiB of HBM per device.

```python
import math
import jax
import jax.numpy as jnp
import numpy as np
from jax import lax

D = 3584
FF = 2048
HEADS = 32
LATENT = 512
ROPE = 64
EXPERTS = 8
TOP = 2
TOK_DEV = 8
CAP = 2
GROUP = 1024
CTX = 8192
N_SECTION = 4
N_EXPERT = 128


def cache_fields(key, low_scale, high_scale):
    key_lat, key_rot, key_scale = jax.random.split(key, 3)
    latent = jax.random.normal(key_lat, (N_SECTION, CTX, LATENT), jnp.float32)
    rotary = jax.random.normal(key_rot, (N_SECTION, CTX, ROPE), jnp.float32)
    joined = jnp.concatenate([latent, rotary], axis=2)
    scales = jnp.exp(jax.random.uniform(key_scale, (N_SECTION, CTX // 2, 1, 1), jnp.float32, math.log(low_scale), math.log(high_scale)))
    paired = joined.reshape(N_SECTION, CTX // 2, 2, LATENT + ROPE)
    second = paired[:, :, 1]
    paired = jnp.stack([paired[:, :, 0], second], axis=2) * scales
    joined = jnp.clip(paired.reshape(N_SECTION, CTX, LATENT + ROPE), -4.0, 4.0)
    return (joined[:, :, :LATENT], joined[:, :, LATENT:])


def draw_cache_latent(key, part):
    latent, rotary = cache_fields(key, 1.0, 1.0)
    return latent.astype(jnp.bfloat16)


def draw_cache_rope(key, part):
    latent, rotary = cache_fields(key, 1.0, 1.0)
    return rotary.astype(jnp.bfloat16)


def draw_query_latent(key, part):
    own_key = jax.random.fold_in(key, 11)
    queries = 0.5 * jnp.clip(jax.random.normal(own_key, (N_SECTION, GROUP, HEADS, LATENT), jnp.float32), -4.0, 4.0)
    return queries.astype(jnp.bfloat16)


def draw_query_rope(key, part):
    own_key = jax.random.fold_in(key, 23)
    queries = jnp.clip(jax.random.normal(own_key, (N_SECTION, GROUP, HEADS * ROPE), jnp.float32), -4.0, 4.0)
    return queries.astype(jnp.bfloat16)


def place_ends(result, key, smallest, largest):
    longest = result.shape.index(max(result.shape))
    spots = []
    for shift in (0, 1):
        where = [jax.random.randint(jax.random.fold_in(key, axis), (), 0, length) for axis, length in enumerate(result.shape)]
        where[longest] = (where[longest] + shift) % result.shape[longest]
        spots.append(tuple(where))
    return result.at[spots[0]].set(smallest).at[spots[1]].set(largest)


def levels(key, extent, cuts, smallest, top_value):
    def one(position, blocks):
        steps = jax.random.uniform(jax.random.fold_in(jax.random.fold_in(key, 6), position), (blocks,), jnp.float32, smallest / len(cuts), top_value / len(cuts))
        return jnp.repeat(jnp.exp(steps), extent[position] // blocks).reshape((-1,) + (1,) * (len(extent) - position - 1))

    level = one(*cuts[0])
    for cut in cuts[1:]:
        level = level * one(*cut)
    return level


def assign_block(rng, own, number, rows, number_of, top, bound, lean):
    ranking = jax.random.permutation(rng, number_of)
    heavy_load, ordinary = portions_of(number_of, rows * top, bound, lean, True), portions_of(number_of, rows * top, bound, lean, False)
    places = jnp.arange(number_of)

    def named(lengths, rotation):
        used = int((lengths > 0).sum())
        fixed = max(1, used // 4)
        moved = fixed + (places - fixed + rotation * (used - fixed)) % max(1, number_of - fixed)
        return jnp.zeros((number_of,), jnp.int32).at[ranking[jnp.where(places < fixed, places, moved)]].set(jnp.asarray(lengths, jnp.int32))

    lengths = jnp.where(number % 4 == 0, named(heavy_load, number // 4), named(ordinary, number - number // 4 - 1))
    mixed = jax.random.permutation(jax.random.fold_in(own, 3), number_of)
    giver, receiver = mixed[0:number_of // 2 * 2:2], mixed[1:number_of // 2 * 2:2]
    slack = jnp.minimum(lengths[giver] - 1, bound - lengths[receiver]) // 2
    slack = jnp.where((giver == ranking[0]) | (receiver == ranking[0]) | (lengths[receiver] == 0), 0, jnp.maximum(slack, 0))
    moved = jax.random.randint(jax.random.fold_in(own, 4), (number_of // 2,), 0, 1 << 20) % (slack + 1)
    lengths = lengths.at[giver].add(-moved).at[receiver].add(moved)
    items = jnp.searchsorted(jnp.cumsum(lengths), jnp.arange(rows * top), side="right").astype(jnp.int32)
    grid = items.reshape(top, rows).T
    grid = grid[jax.random.permutation(jax.random.fold_in(own, 1), rows)]
    rotation = jax.random.randint(jax.random.fold_in(own, 2), (rows, 1), 0, top)
    return jnp.take_along_axis(grid, (jnp.arange(top)[None, :] + rotation) % top, axis=1)


def portions_of(number_of, total, most, skew, full):
    loads = [(1 << 20) // math.isqrt(rank ** skew) + 1 for rank in range(1, number_of + 1)]
    largest = most if full else min(most, max(-(-total // number_of), total * loads[0] // sum(loads)))
    least = 1 if total - largest >= number_of - 1 else 0
    holding, spare = [largest] + [least] * (number_of - 1), total - largest - least * (number_of - 1)
    while spare > 0:
        movable = [i for i in range(1, number_of) if holding[i] < largest] or [i for i in range(1, number_of) if holding[i] < most]
        whole, remaining = sum([loads[i] for i in movable]), spare
        for i in movable:
            extra = min(most - holding[i], max(1, remaining * loads[i] // whole), spare)
            holding[i] = holding[i] + extra
            spare = spare - extra
    return np.array(holding)


def normal_values(rng, dims, spread, reach, cuts=(), held_as=jnp.bfloat16):
    array = spread * jax.random.normal(rng, dims, jnp.float32)
    if cuts:
        array = array * levels(rng, dims, cuts, -0.22, 0.18)
    return jnp.clip(array, -reach, reach).astype(held_as)


def setup_inputs(seed: int = 0) -> dict:
    arg_keys = jax.random.split(jax.random.key(seed), 12)
    hidden_rows = normal_values(arg_keys[0], (N_SECTION, GROUP, D), 1.0, 6.0, ((0, 4), (1, 128)))
    expert_ids_keys = jax.random.split(jax.random.fold_in(arg_keys[1], 1), N_SECTION * GROUP // TOK_DEV)
    expert_ids_turns = jax.random.permutation(jax.random.fold_in(arg_keys[1], 3), N_SECTION * GROUP // TOK_DEV)
    expert_ids = jax.vmap(lambda own, number: assign_block(jax.random.fold_in(arg_keys[1], 2), own, number, TOK_DEV, EXPERTS, TOP, CAP, 2))(expert_ids_keys, expert_ids_turns).reshape((N_SECTION, GROUP, TOP))
    gate_weights = jnp.clip(jnp.exp(math.log(2.0) - 2.3025851 * jax.random.uniform(arg_keys[2], (N_SECTION, GROUP, TOP), jnp.float32) ** levels(arg_keys[2], (N_SECTION, GROUP, TOP), ((0, 4), (1, 128)), -0.2, 0.2)), 0.2, 2.0)
    w_gate = normal_values(arg_keys[3], (N_SECTION, D, EXPERTS * FF), D ** -0.5, 0.09375, ((0, 4), (2, 128)))
    w_up = normal_values(arg_keys[4], (N_SECTION, D, EXPERTS * FF), D ** -0.5, 0.09375, ((0, 4), (2, 128)))
    w_down = normal_values(arg_keys[5], (N_SECTION, EXPERTS * FF, D), FF ** -0.5, 0.125, ((0, 4), (1, 128)))
    query_latent = draw_query_latent(jax.random.fold_in(arg_keys[11], 71), 0)
    query_rope = draw_query_rope(jax.random.fold_in(arg_keys[11], 71), 0)
    cache_latent = draw_cache_latent(jax.random.fold_in(arg_keys[11], 71), 0)
    cache_rope = draw_cache_rope(jax.random.fold_in(arg_keys[11], 71), 0)
    offsets = place_ends(jax.random.randint(arg_keys[10], (N_SECTION,), 0, CTX - GROUP + 1), jax.random.fold_in(arg_keys[10], 1), 0, CTX - GROUP).astype(jnp.int32)
    return dict(hidden_rows=hidden_rows, expert_ids=expert_ids, gate_weights=gate_weights, w_gate=w_gate, w_up=w_up, w_down=w_down, query_latent=query_latent, query_rope=query_rope, cache_latent=cache_latent, cache_rope=cache_rope, offsets=offsets)


softmax_scale = 192.0 ** -0.5
masked_score = -1.0e30


def attend_section(query_lat, query_rot, cache_lat, cache_rot, first_pos):
    group_rows, head_count, latent_width = query_lat.shape
    rot_heads = query_rot.reshape(group_rows, head_count, -1).astype(jnp.float32)
    lat_query = query_lat.astype(jnp.float32)
    keys_lat = cache_lat.astype(jnp.float32)
    keys_rot = cache_rot.astype(jnp.float32)
    block_rows = math.gcd(256, group_rows)
    key_pos = jnp.arange(cache_lat.shape[0], dtype=jnp.int32)

    def one_block(block_index):
        first_row = block_index * block_rows
        block_lat = lax.dynamic_slice_in_dim(lat_query, first_row, block_rows, 0)
        block_rot = lax.dynamic_slice_in_dim(rot_heads, first_row, block_rows, 0)
        scores = jnp.einsum("thl,jl->thj", block_lat, keys_lat, precision=lax.Precision.HIGHEST)
        scores = scores + jnp.einsum("thr,jr->thj", block_rot, keys_rot, precision=lax.Precision.HIGHEST)
        scores = scores * softmax_scale
        positions = first_pos + first_row + jnp.arange(block_rows, dtype=jnp.int32)
        visible = key_pos[None, None, :] <= positions[:, None, None]
        highest = jnp.max(jnp.where(visible, scores, masked_score), axis=2, keepdims=True)
        weights = jnp.where(visible, jnp.exp(jnp.where(visible, scores - highest, masked_score)), 0.0)
        totals = jnp.sum(weights, axis=2)
        rounded = lax.optimization_barrier(weights.astype(jnp.bfloat16)).astype(jnp.float32)
        summed = jnp.einsum("thj,jl->thl", rounded, keys_lat, precision=lax.Precision.HIGHEST)
        return (summed / totals[:, :, None]).astype(jnp.bfloat16)

    blocks = lax.map(one_block, jnp.arange(group_rows // block_rows, dtype=jnp.int32))
    return blocks.reshape(group_rows, head_count, latent_width)


def experts_section(tokens, routing, gate_share, gate_weight, up_weight, down_weight):
    group_rows, model_width = tokens.shape
    slices = N_EXPERT // EXPERTS
    hidden_width = FF // slices
    row_bound = min(group_rows, N_EXPERT * CAP)
    expert_range = jnp.arange(EXPERTS, dtype=jnp.int32)
    matches = routing[:, :, None] == expert_range[None, None, :]
    chosen = jnp.any(matches, axis=1).astype(jnp.int32)
    gate_of = jnp.sum(jnp.where(matches, gate_share[:, :, None], 0.0), axis=1)

    def one_expert(mixture, expert):
        routed = chosen[:, expert]
        picked_order = jnp.argsort(1 - routed, stable=True)[:row_bound].astype(jnp.int32)
        picked = tokens[picked_order]
        first_col = expert * FF
        gate_cols = lax.dynamic_slice_in_dim(gate_weight, first_col, FF, 1)
        up_cols = lax.dynamic_slice_in_dim(up_weight, first_col, FF, 1)
        down_rows = lax.dynamic_slice_in_dim(down_weight, first_col, FF, 0)
        gate_val = jnp.dot(picked, gate_cols, preferred_element_type=jnp.float32)
        up_val = jnp.dot(picked, up_cols, preferred_element_type=jnp.float32)
        activated = (jax.nn.silu(gate_val) * up_val).astype(jnp.bfloat16)
        blocks_in = activated.reshape(row_bound, slices, hidden_width).astype(jnp.float32)
        blocks_weight = down_rows.reshape(slices, hidden_width, model_width).astype(jnp.float32)
        pieces = jnp.einsum("rsh,shd->rsd", blocks_in, blocks_weight, precision=lax.Precision.HIGHEST).astype(jnp.bfloat16)
        summed = jnp.sum(pieces.astype(jnp.float32), axis=1)
        gate_scale = gate_of[picked_order, expert] * routed[picked_order].astype(jnp.float32)
        return mixture.at[picked_order].add(summed * gate_scale[:, None]), None

    mixture, ignored = lax.scan(one_expert, jnp.zeros((group_rows, model_width), jnp.float32), expert_range)
    return mixture


def reference(hidden_rows, expert_ids, gate_weights, w_gate, w_up, w_down, query_latent, query_rope, cache_latent, cache_rope, offsets):
    results = []
    attended = []
    for section_index in range(N_SECTION):
        mixture = experts_section(hidden_rows[section_index], expert_ids[section_index], gate_weights[section_index], w_gate[section_index], w_up[section_index], w_down[section_index])
        results.append((hidden_rows[section_index].astype(jnp.float32) + mixture).astype(jnp.bfloat16))
        attended.append(attend_section(query_latent[section_index], query_rope[section_index], cache_latent[section_index], cache_rope[section_index], offsets[section_index]))
    passed = jnp.stack([results[(section_index - 1) % N_SECTION] for section_index in range(N_SECTION)])
    return passed, jnp.stack(attended)
```

```python
import functools
import math

import jax
import jax.numpy as jnp
from jax import lax
from jax.experimental import pallas as pl
from jax.experimental.pallas import tpu as pltpu
from jax.sharding import PartitionSpec as P

MESH = pl.DeviceIdType.MESH
EXPERTS = 8
NZ, NY = 16, 4
TOKENS, HEADS = 8, 32
ROWS = TOKENS * HEADS
LATENT, ROPE = 512, 64
KEYS = 64
KW = LATENT + 128
WIDTH = 3584
COLS = WIDTH // NY
HALF = NZ // 2
NEAR = NZ // 4
scale_log2 = 192.0 ** (-0.5) * math.log2(math.e)
masked_score = -1e30
f32, bf16 = jnp.float32, jnp.bfloat16


def slot_of(r):
    return (r + NEAR) % NZ


def kernel(
    x_ref, ids_ref, gate_ref, wg_ref, wu_ref, wd_ref, q_ref, qrope_ref, klat_ref, krope_ref, offset_ref,
    passed_ref, out_ref,
    kbuf, ql, qraw, qr, rel, acc, m_ref, l_ref, o_send, o_recv, ls_send, ls_recv,
    xs, xs_recv, g_recv, packed, xall, wgu, wd, csib_send, csib_recv, own_sum, cy_send, cy_recv, csum, ret, fin, fin_recv,
    send_ring, recv_ring, send_sib, recv_sib, send_q, recv_q, send_o, recv_o,
    send_d1, recv_d1, send_d2, recv_d2, send_d3, recv_d3, send_d3s, recv_d3s,
    send_c0, recv_c0, send_c1, recv_c1, send_c2, recv_c2, send_fin, recv_fin, sem_w, sem_l,
):
    sec = lax.axis_index("section")
    nsec = lax.axis_size("section")
    me = lax.axis_index("expert")
    c = lax.rem(me, 2)
    y = lax.rem(lax.div(me, 2), NY)
    z = lax.div(me, 2 * NY)
    sib = me + 1 - 2 * c

    def at(zz, yy):
        return (sec, (zz * NY + yy) * 2 + c)

    def zplus(r):
        return lax.rem(z + (r % NZ), NZ)

    def yplus(d):
        return lax.rem(y + (d % NY), NY)

    next_sec = lax.rem(sec + 1, nsec)
    prev_sec = lax.rem(sec + nsec - 1, nsec)
    sends = []

    def send(src, dst, ssem, rsem, device):
        copy = pltpu.make_async_remote_copy(
            src_ref=src, dst_ref=dst, send_sem=ssem, recv_sem=rsem, device_id=device, device_id_type=MESH
        )
        copy.start()
        sends.append(copy)

    def arrived(ref, sem):
        pltpu.make_async_copy(ref, ref, sem).wait()

    barrier = pltpu.get_barrier_semaphore()

    def greet(device):
        pl.semaphore_signal(barrier, inc=1, device_id=device, device_id_type=MESH)

    greet((sec, sib))
    for d in range(1, NY):
        greet(at(z, yplus(d)))
    for r in range(1, NZ):
        greet(at(zplus(r), y))
    for d in range(NY):
        greet((prev_sec, (z * NY + d) * 2 + c))

    locals_ = [pltpu.make_async_copy(q_ref, ql.at[0], sem_l.at[0])]
    for k in range(NY):
        rows = pl.ds(k * COLS, COLS)
        locals_.append(pltpu.make_async_copy(wg_ref.at[rows, :], wgu.at[k, :, pl.ds(0, 128)], sem_w.at[k, 0]))
        locals_.append(pltpu.make_async_copy(wu_ref.at[rows, :], wgu.at[k, :, pl.ds(128, 128)], sem_w.at[k, 1]))
        locals_.append(pltpu.make_async_copy(wd_ref.at[:, rows], wd.at[k], sem_w.at[k, 2]))
    for copy in locals_:
        copy.start()

    for k in range(NY):
        xs[k] = x_ref[:, k * COLS : (k + 1) * COLS]
    kbuf[0, 0, :, :LATENT] = klat_ref[...]
    kbuf[0, 0, :, LATENT:] = jnp.concatenate([krope_ref[...], jnp.zeros((KEYS, 128 - ROPE), bf16)], axis=1)

    lane = lax.broadcasted_iota(jnp.int32, (TOKENS, 128), 1)
    token = lax.broadcasted_iota(jnp.int32, (TOKENS, 128), 0)
    lane_e, lane_y, lane_rank = lane >> 3, (lane >> 1) & 3, lane & 1
    first, second = ids_ref[:, 0:1] == lane_e, ids_ref[:, 1:2] == lane_e
    hit = jnp.where(first | second, 1, 0)
    rank = jnp.zeros((TOKENS, 128), jnp.int32)
    for t in range(TOKENS - 1):
        rank = rank + jnp.where(token > t, hit[t : t + 1, :], 0)
    share = jnp.where(first, gate_ref[:, 0:1], gate_ref[:, 1:2])
    g_recv[0] = jnp.where((hit == 1) & (rank == lane_rank) & (lane_y == y), share, 0.0)
    xs_recv[0] = xs[y]

    pl.semaphore_wait(barrier, 1 + (NY - 1) + (NZ - 1) + NY)

    for d in range(1, NY):
        to = at(z, yplus(d))
        send(xs.at[yplus(d)], xs_recv.at[NY - d], send_d1.at[0, d], recv_d1.at[0], to)
        send(g_recv.at[0], g_recv.at[NY - d], send_d1.at[1, d], recv_d1.at[1], to)
    send(kbuf.at[0, 0], kbuf.at[1, 0], send_ring.at[0, 0], recv_ring.at[0, 1], at(zplus(1), y))
    send(kbuf.at[0, 0], kbuf.at[1, 2], send_ring.at[1, 0], recv_ring.at[1, 1], at(zplus(-1), y))
    send(kbuf.at[0, 0], kbuf.at[0, 1], send_sib.at[0, 0], recv_sib.at[0, 0], (sec, sib))
    for d in (1, 3, 2):
        to = at(z, yplus(d))
        send(q_ref, ql.at[NY - d], send_q.at[0, d], recv_q.at[0, NY - d], to)
        send(qrope_ref, qraw.at[NY - d], send_q.at[1, d], recv_q.at[1, NY - d], to)

    arrived(xs_recv.at[pl.ds(1, NY - 1)], recv_d1.at[0])
    arrived(g_recv.at[pl.ds(1, NY - 1)], recv_d1.at[1])
    gates = g_recv[...].reshape(NY * TOKENS, 128)
    pick = jnp.where(jnp.transpose(gates)[: 8 * EXPERTS] != 0.0, 1.0, 0.0).astype(bf16)
    plane = xs_recv[...].astype(f32).reshape(NY * TOKENS, COLS).astype(bf16)
    packed[...] = jnp.dot(pick, plane, preferred_element_type=f32).reshape(EXPERTS, 8, COLS).astype(bf16)
    mine = pltpu.make_async_copy(packed.at[lax.div(z, 2)], xall.at[0, 0, slot_of(0)], recv_d2.at[0])
    mine.start()
    for r in sorted(range(1, NZ), key=lambda r: min(r, NZ - r)):
        slot = slot_of(-r)
        send(
            packed.at[lax.div(zplus(r), 2)], xall.at[0, 0, slot], send_d2.at[r], recv_d2.at[slot // HALF], at(zplus(r), y)
        )

    def ring(s):
        if s < HALF:
            arrived(kbuf.at[s, 0], recv_ring.at[0, s])
            arrived(kbuf.at[s, 2], recv_ring.at[1, s])
            if s < HALF - 1:
                send(kbuf.at[s, 0], kbuf.at[s + 1, 0], send_ring.at[0, s], recv_ring.at[0, s + 1], at(zplus(1), y))
                send(kbuf.at[s, 2], kbuf.at[s + 1, 2], send_ring.at[1, s], recv_ring.at[1, s + 1], at(zplus(-1), y))
            else:
                low, high = pl.ds(0, KEYS // 2), pl.ds(KEYS // 2, KEYS // 2)
                send(
                    kbuf.at[s, 0, low], kbuf.at[0, 2, low], send_ring.at[0, s], recv_ring.at[0, s + 1], at(zplus(1), y)
                )
                send(
                    kbuf.at[s, 2, high], kbuf.at[0, 2, high], send_ring.at[1, s], recv_ring.at[1, s + 1], at(zplus(-1), y)
                )
            send(kbuf.at[s, 0], kbuf.at[s, 1], send_sib.at[0, s], recv_sib.at[0, s], (sec, sib))
            send(kbuf.at[s, 2], kbuf.at[s, 3], send_sib.at[1, s], recv_sib.at[1, s], (sec, sib))
        else:
            arrived(kbuf.at[0, 2, pl.ds(0, KEYS // 2)], recv_ring.at[0, s])
            arrived(kbuf.at[0, 2, pl.ds(KEYS // 2, KEYS // 2)], recv_ring.at[1, s])
            send(kbuf.at[0, 2], kbuf.at[0, 3], send_sib.at[1, 0], recv_sib.at[1, 0], (sec, sib))

    def spread_rope():
        keep = lax.broadcasted_iota(jnp.int32, (TOKENS, 128), 1) < ROPE

        def one(d, carry):
            for h in range(HEADS):
                pair = qraw[d, :, (h // 2) * 128 : (h // 2 + 1) * 128].astype(f32)
                if h % 2:
                    pair = pltpu.roll(pair, ROPE, 1)
                rel[pl.ds(h, TOKENS, stride=HEADS), :] = jnp.where(keep, pair, 0.0)
            qr[d] = rel[...].astype(bf16)
            return carry

        lax.fori_loop(0, NY, one, 0)

    def attend(s, first):
        arrived(kbuf.at[s, 1], recv_sib.at[0, s])
        arrived(kbuf.at[s, 3], recv_sib.at[1, s])
        lanes = lax.broadcasted_iota(jnp.int32, (1, 1, 4 * KEYS), 2)
        block, inside = lanes // KEYS, lanes % KEYS
        za, zb = (z, zplus(HALF)) if s == 0 else (zplus(-s), zplus(s))
        zz = jnp.where(block < 2, za, zb)
        cc = jnp.where(block % 2 == 0, c, 1 - c)
        key_pos = ((zz * NY + y) * 2 + cc) * KEYS + inside
        kc = kbuf[s].reshape(4 * KEYS, KW)
        k_lat, k_rope = kc[:, :LATENT], kc[:, LATENT:]
        token_of = lax.broadcasted_iota(jnp.int32, (TOKENS, 1, 1), 0)

        def one(d, carry):
            owner = (z * NY + lax.rem(y + d, NY)) * 2 + c
            position = offset_ref[0] + owner * TOKENS + token_of
            cap = jnp.where(key_pos <= position, jnp.inf, masked_score)
            contract = (((1,), (1,)), ((), ()))
            score = lax.dot_general(ql[d], k_lat, contract, preferred_element_type=f32)
            score = score + lax.dot_general(qr[d], k_rope, contract, preferred_element_type=f32)
            score = jnp.minimum(score.reshape(TOKENS, HEADS, 4 * KEYS), cap).reshape(ROWS, 4 * KEYS)
            left, right = score[:, :128], score[:, 128:]
            top = jnp.max(jnp.maximum(left, right), axis=1, keepdims=True)
            if first:
                new = jnp.broadcast_to(top, (ROWS, 128))
            else:
                old = m_ref[d]
                new = jnp.maximum(old, top)
                alpha = jnp.exp2((old - new) * scale_log2)
            left = jnp.exp2((left - new) * scale_log2)
            right = jnp.exp2((right - new) * scale_log2)
            weights = jnp.concatenate([left.astype(bf16), right.astype(bf16)], axis=1)
            value = jnp.dot(weights, k_lat, preferred_element_type=f32)
            m_ref[d] = new
            if first:
                l_ref[d] = left + right
                acc[d] = value
            else:
                l_ref[d] = l_ref[d] * alpha + left + right
                acc[d] = acc[d] * jnp.concatenate([alpha] * (LATENT // 128), axis=1) + value
            return carry

        lax.fori_loop(0, NY, one, 0)

    def spread(half):
        part = pl.ds(half * HALF, HALF)
        arrived(xall.at[0, 0, part], recv_d2.at[half])
        for d in (1, 3, 2):
            send(
                xall.at[0, 0, part], xall.at[NY - d, 0, part], send_d3.at[half, d], recv_d3.at[half, NY - d],
                at(z, yplus(d)),
            )
        send(xall.at[0, 0, part], xall.at[0, 1, part], send_d3s.at[half, 0], recv_d3s.at[half, 0], (sec, sib))

    def share_rows(half):
        part = pl.ds(half * HALF, HALF)
        for d in (1, 3, 2):
            arrived(xall.at[d, 0, part], recv_d3.at[half, d])
            send(xall.at[d, 0, part], xall.at[d, 1, part], send_d3s.at[half, d], recv_d3s.at[half, d], (sec, sib))

    n_rows = HALF * 8

    def experts(half):
        part = pl.ds(half * HALF, HALF)
        total = None
        for d in range(NY):
            arrived(xall.at[d, 1, part], recv_d3s.at[half, d])
            rows = xall[d, :, half * HALF : (half + 1) * HALF].astype(f32).reshape(2 * n_rows, COLS).astype(bf16)
            term = jnp.dot(rows, wgu[yplus(d)], preferred_element_type=f32)
            total = term if total is None else total + term
        gate, up = total[:, :128], total[:, 128:]
        active = (gate / (1.0 + jnp.exp(-gate)) * up).astype(bf16)
        for d in range(NY):
            piece = jnp.dot(active, wd[yplus(d)], preferred_element_type=f32).reshape(2, HALF, 8, COLS)
            own_sum[half, d] = piece[0]
            csib_send[half, d] = piece[1].astype(bf16)
        send(csib_send.at[half], csib_recv.at[half], send_c0.at[half], recv_c0.at[half], (sec, sib))

    def combine(half):
        arrived(csib_recv.at[half], recv_c0.at[half])
        for d in (1, 3, 2):
            cy_send[half, d - 1] = (own_sum[half, d] + csib_recv[half, d].astype(f32)).astype(bf16)
            send(
                cy_send.at[half, d - 1], cy_recv.at[half, NY - d - 1], send_c1.at[half, d], recv_c1.at[half, NY - d],
                at(z, yplus(d)),
            )

    def give_back(half):
        total = own_sum[half, 0] + csib_recv[half, 0].astype(f32)
        for d in range(1, NY):
            arrived(cy_recv.at[half, d - 1], recv_c1.at[half, d])
            total = total + cy_recv[half, d - 1].astype(f32)
        csum[half] = total.astype(bf16)
        for slot in range(half * HALF, (half + 1) * HALF):
            r = (slot - NEAR) % NZ
            block = csum.at[half, slot - half * HALF]
            if r == 0:
                back = pltpu.make_async_copy(block, ret.at[z], recv_c2)
                back.start()
            else:
                send(block, ret.at[z], send_c2.at[r], recv_c2, at(zplus(r), y))

    def finish():
        arrived(ret, recv_c2)
        pairs = ret[...].astype(f32).reshape(EXPERTS, 2, 8, COLS)
        rows = (pairs[:, 0] + pairs[:, 1]).reshape(8 * EXPERTS, COLS)
        weights = g_recv[...].reshape(NY * TOKENS, 128)[:, : 8 * EXPERTS]
        mixture = jnp.dot(weights, rows, precision=lax.Precision.HIGHEST, preferred_element_type=f32)
        result = mixture.reshape(NY, TOKENS, COLS) + xs_recv[...].astype(f32)
        fin[...] = result.astype(bf16)
        for d in range(NY):
            to = (next_sec, (z * NY + yplus(d)) * 2 + c)
            send(fin.at[d], fin_recv.at[y], send_fin.at[d], recv_fin, to)

    def close(d):
        total = jnp.sum(l_ref[d], axis=1, keepdims=True)
        level = m_ref[d] * scale_log2 + jnp.log2(total)
        return level, acc[d] / total

    def give_out():
        for d in (2, 1, 3):
            level, value = close(d)
            o_send[d - 1] = value.astype(bf16)
            ls_send[d - 1] = jnp.transpose(level)[:8, :]
            to = at(z, yplus(d))
            send(o_send.at[d - 1], o_recv.at[NY - d - 1], send_o.at[0, d], recv_o.at[0, NY - d], to)
            send(ls_send.at[d - 1], ls_recv.at[NY - d - 1], send_o.at[1, d], recv_o.at[1, NY - d], to)

    def merge():
        level, value = close(0)
        levels, values = [level], [value]
        for d in range(1, NY):
            arrived(o_recv.at[d - 1], recv_o.at[0, d])
            arrived(ls_recv.at[d - 1], recv_o.at[1, d])
            levels.append(jnp.transpose(jnp.broadcast_to(ls_recv[d - 1][0:1, :], (128, ROWS))))
        best = functools.reduce(jnp.maximum, levels)
        shares = [jnp.exp2(one - best) for one in levels]
        norm = 1.0 / functools.reduce(jnp.add, shares)
        total = value * jnp.concatenate([shares[0] * norm] * (LATENT // 128), axis=1)
        for d in range(1, NY):
            factor = jnp.concatenate([shares[d] * norm] * (LATENT // 128), axis=1)
            total = total + o_recv[d - 1].astype(f32) * factor
        out_ref[...] = total.astype(bf16)

    ring(1)
    ring(2)
    spread(0)
    qraw[0] = qrope_ref[...]
    ring(3)
    for d in (1, 3, 2):
        arrived(ql.at[d], recv_q.at[0, d])
        arrived(qraw.at[d], recv_q.at[1, d])
    locals_[0].wait()
    spread_rope()
    ring(4)
    attend(1, True)
    spread(1)
    ring(5)
    share_rows(0)
    attend(2, False)
    ring(6)
    for copy in locals_[1:]:
        copy.wait()
    experts(0)
    ring(7)
    attend(3, False)
    combine(0)
    ring(8)
    share_rows(1)
    attend(4, False)
    experts(1)
    attend(5, False)
    combine(1)
    give_back(0)
    attend(6, False)
    attend(7, False)
    attend(0, False)
    give_back(1)
    give_out()
    finish()
    merge()
    arrived(fin_recv, recv_fin)
    for k in range(NY):
        passed_ref[:, k * COLS : (k + 1) * COLS] = fin_recv[k]
    for copy in sends:
        copy.wait_send()


def per_device(
    hidden_rows, expert_ids, gate_weights, w_gate, w_up, w_down, query_latent, query_rope, cache_latent, cache_rope, offsets
):
    vmem = pl.BlockSpec(memory_space=pltpu.VMEM)
    anywhere = pl.BlockSpec(memory_space=pl.ANY)
    dma = pltpu.SemaphoreType.DMA
    passed, attended = pl.pallas_call(
        kernel,
        out_shape=(
            jax.ShapeDtypeStruct((TOKENS, WIDTH), bf16),
            jax.ShapeDtypeStruct((ROWS, LATENT), bf16),
        ),
        in_specs=[
            vmem, vmem, vmem, anywhere, anywhere, anywhere, anywhere, vmem, vmem, vmem,
            pl.BlockSpec(memory_space=pltpu.SMEM),
        ],
        out_specs=(vmem, vmem),
        scratch_shapes=[
            pltpu.VMEM((HALF, 4, KEYS, KW), bf16),
            pltpu.VMEM((NY, ROWS, LATENT), bf16),
            pltpu.VMEM((NY, TOKENS, HEADS * ROPE), bf16),
            pltpu.VMEM((NY, ROWS, 128), bf16),
            pltpu.VMEM((ROWS, 128), f32),
            pltpu.VMEM((NY, ROWS, LATENT), f32),
            pltpu.VMEM((NY, ROWS, 128), f32),
            pltpu.VMEM((NY, ROWS, 128), f32),
            pltpu.VMEM((NY - 1, ROWS, LATENT), bf16),
            pltpu.VMEM((NY - 1, ROWS, LATENT), bf16),
            pltpu.VMEM((NY - 1, 8, ROWS), f32),
            pltpu.VMEM((NY - 1, 8, ROWS), f32),
            pltpu.VMEM((NY, TOKENS, COLS), bf16),
            pltpu.VMEM((NY, TOKENS, COLS), bf16),
            pltpu.VMEM((NY, TOKENS, 128), f32),
            pltpu.VMEM((EXPERTS, 8, COLS), bf16),
            pltpu.VMEM((NY, 2, NZ, 8, COLS), bf16),
            pltpu.VMEM((NY, COLS, 256), bf16),
            pltpu.VMEM((NY, 128, COLS), bf16),
            pltpu.VMEM((2, NY, HALF, 8, COLS), bf16),
            pltpu.VMEM((2, NY, HALF, 8, COLS), bf16),
            pltpu.VMEM((2, NY, HALF, 8, COLS), f32),
            pltpu.VMEM((2, NY - 1, HALF, 8, COLS), bf16),
            pltpu.VMEM((2, NY - 1, HALF, 8, COLS), bf16),
            pltpu.VMEM((2, HALF, 8, COLS), bf16),
            pltpu.VMEM((NZ, 8, COLS), bf16),
            pltpu.VMEM((NY, TOKENS, COLS), bf16),
            pltpu.VMEM((NY, TOKENS, COLS), bf16),
            dma((2, HALF)), dma((2, HALF + 1)),
            dma((2, HALF)), dma((2, HALF)),
            dma((2, NY)), dma((2, NY)),
            dma((2, NY)), dma((2, NY)),
            dma((2, NY)), dma((2,)),
            dma((NZ,)), dma((2,)),
            dma((2, NY)), dma((2, NY)),
            dma((2, NY)), dma((2, NY)),
            dma((2,)), dma((2,)),
            dma((2, NY)), dma((2, NY)),
            dma((NZ,)), dma,
            dma((NY,)), dma,
            dma((NY, 3)), dma((1,)),
        ],
        compiler_params=pltpu.CompilerParams(
            collective_id=0, has_side_effects=True, vmem_limit_bytes=56 * 1024 * 1024
        ),
        cost_estimate=pl.CostEstimate(flops=6_000_000_000, bytes_accessed=4_000_000, transcendentals=2_000_000),
        name="layer",
    )(
        hidden_rows[0], expert_ids[0], gate_weights[0], w_gate[0], w_up[0], w_down[0],
        query_latent.reshape(ROWS, LATENT), query_rope[0], cache_latent[0], cache_rope[0], offsets,
    )
    return passed[None], attended.reshape(1, TOKENS, HEADS, LATENT)


def solution(mesh):
    rows = P("section", "expert", None)
    heads = P("section", "expert", None, None)
    return jax.shard_map(
        per_device,
        mesh=mesh,
        in_specs=(rows, rows, rows, P("section", None, "expert"), P("section", None, "expert"), rows, heads, rows, rows, rows, P("section")),
        out_specs=(rows, heads),
        check_vma=False,
    )
```

```python
import functools
import math

import jax
import jax.numpy as jnp
from jax import lax
from jax.experimental import pallas as pl
from jax.experimental.pallas import tpu as pltpu
from jax.sharding import PartitionSpec as P

MESH = pl.DeviceIdType.MESH
EXPERTS = 8
NZ, NY = 16, 4
TOKENS, HEADS = 8, 32
ROWS = TOKENS * HEADS
LATENT, ROPE = 512, 64
KEYS = 64
KW = LATENT + 128
WIDTH = 3584
COLS = WIDTH // NY
HALF = NZ // 2
scale_log2 = 192.0 ** (-0.5) * math.log2(math.e)
masked_score = -1e30
f32, bf16 = jnp.float32, jnp.bfloat16


def kernel(
    x_ref, ids_ref, gate_ref, wg_ref, wu_ref, wd_ref, q_ref, qrope_ref, klat_ref, krope_ref, offset_ref,
    passed_ref, out_ref,
    kbuf, ql, qraw, qr, rel, acc, m_ref, l_ref, o_send, o_recv, ls_send, ls_recv,
    xs, xs_recv, g_recv, packed, xall, wgu, wd, csib_send, csib_recv, own_sum, cy_send, cy_recv, csum, ret, fin, fin_recv,
    send_ring, recv_ring, send_sib, recv_sib, send_q, recv_q, send_o, recv_o,
    send_d1, recv_d1, send_d2, recv_d2, send_d3, recv_d3, send_d3s, recv_d3s,
    send_c0, recv_c0, send_c1, recv_c1, send_c2, recv_c2, send_fin, recv_fin, sem_w, sem_l,
):
    sec = lax.axis_index("section")
    nsec = lax.axis_size("section")
    me = lax.axis_index("expert")
    c = lax.rem(me, 2)
    y = lax.rem(lax.div(me, 2), NY)
    z = lax.div(me, 2 * NY)
    sib = me + 1 - 2 * c

    def at(zz, yy):
        return (sec, (zz * NY + yy) * 2 + c)

    def zplus(r):
        return lax.rem(z + (r % NZ), NZ)

    def yplus(d):
        return lax.rem(y + (d % NY), NY)

    side = lax.rem(z, 2)
    outward = 2 * side - 1
    pair = at(z - outward, y)
    next_sec = lax.rem(sec + 1, nsec)
    prev_sec = lax.rem(sec + nsec - 1, nsec)
    sends = []

    def send(src, dst, ssem, rsem, device):
        copy = pltpu.make_async_remote_copy(
            src_ref=src, dst_ref=dst, send_sem=ssem, recv_sem=rsem, device_id=device, device_id_type=MESH
        )
        copy.start()
        sends.append(copy)

    def arrived(ref, sem):
        pltpu.make_async_copy(ref, ref, sem).wait()

    barrier = pltpu.get_barrier_semaphore()

    def greet(device):
        pl.semaphore_signal(barrier, inc=1, device_id=device, device_id_type=MESH)

    greet((sec, sib))
    for d in range(1, NY):
        greet(at(z, yplus(d)))
    for r in range(1, NZ):
        greet(at(zplus(r), y))
    for d in range(NY):
        greet((prev_sec, (z * NY + d) * 2 + c))

    locals_ = [pltpu.make_async_copy(q_ref, ql.at[0], sem_l.at[0])]
    for k in range(NY):
        rows = pl.ds(k * COLS, COLS)
        locals_.append(pltpu.make_async_copy(wg_ref.at[rows, :], wgu.at[k, :, pl.ds(0, 128)], sem_w.at[k, 0]))
        locals_.append(pltpu.make_async_copy(wu_ref.at[rows, :], wgu.at[k, :, pl.ds(128, 128)], sem_w.at[k, 1]))
        locals_.append(pltpu.make_async_copy(wd_ref.at[:, rows], wd.at[k], sem_w.at[k, 2]))
    for copy in locals_:
        copy.start()

    for k in range(NY):
        xs[k] = x_ref[:, k * COLS : (k + 1) * COLS]
    kbuf[0, 0, :, :LATENT] = klat_ref[...]
    kbuf[0, 0, :, LATENT:] = jnp.concatenate([krope_ref[...], jnp.zeros((KEYS, 128 - ROPE), bf16)], axis=1)

    lane = lax.broadcasted_iota(jnp.int32, (TOKENS, 128), 1)
    token = lax.broadcasted_iota(jnp.int32, (TOKENS, 128), 0)
    lane_e, lane_y, lane_rank = lane >> 3, (lane >> 1) & 3, lane & 1
    first, second = ids_ref[:, 0:1] == lane_e, ids_ref[:, 1:2] == lane_e
    hit = jnp.where(first | second, 1, 0)
    rank = jnp.zeros((TOKENS, 128), jnp.int32)
    for t in range(TOKENS - 1):
        rank = rank + jnp.where(token > t, hit[t : t + 1, :], 0)
    share = jnp.where(first, gate_ref[:, 0:1], gate_ref[:, 1:2])
    g_recv[0] = jnp.where((hit == 1) & (rank == lane_rank) & (lane_y == y), share, 0.0)
    xs_recv[0] = xs[y]

    pl.semaphore_wait(barrier, 1 + (NY - 1) + (NZ - 1) + NY)

    for d in range(1, NY):
        to = at(z, yplus(d))
        send(xs.at[yplus(d)], xs_recv.at[NY - d], send_d1.at[0, d], recv_d1.at[0], to)
        send(g_recv.at[0], g_recv.at[NY - d], send_d1.at[1, d], recv_d1.at[1], to)
    onward = 1 - 2 * c
    following = at(lax.rem(z + onward + NZ, NZ), y)
    send(kbuf.at[0, 0], kbuf.at[1, 0], send_ring.at[0, 0], recv_ring.at[1, 0], following)
    send(kbuf.at[0, 0], kbuf.at[0, 1], send_sib.at[0, 0], recv_sib.at[0, 0], (sec, sib))
    for d in (1, 3, 2):
        to = at(z, yplus(d))
        send(q_ref, ql.at[NY - d], send_q.at[0, d], recv_q.at[0, NY - d], to)
        send(qrope_ref, qraw.at[NY - d], send_q.at[1, d], recv_q.at[1, NY - d], to)

    arrived(xs_recv.at[pl.ds(1, NY - 1)], recv_d1.at[0])
    arrived(g_recv.at[pl.ds(1, NY - 1)], recv_d1.at[1])
    gates = g_recv[...].reshape(NY * TOKENS, 128)
    pick = jnp.where(jnp.transpose(gates)[: 8 * EXPERTS] != 0.0, 1.0, 0.0).astype(bf16)
    plane = xs_recv[...].astype(f32).reshape(NY * TOKENS, COLS).astype(bf16)
    packed[...] = jnp.dot(pick, plane, preferred_element_type=f32).reshape(EXPERTS, 8, COLS).astype(bf16)
    mine = pltpu.make_async_copy(packed.at[lax.div(z, 2)], xall.at[0, 0, 0, 0], recv_d2)
    mine.start()
    for i in (4, 3, 5, 2, 6, 1, 7):
        e = lax.rem(lax.div(z, 2) + i, EXPERTS)
        delta = 2 * i - side
        far = lax.div(delta, HALF)
        u = delta + far * (NZ - 1 - 2 * delta)
        send(packed.at[e], xall.at[0, 0, 0, u], send_d2.at[i], recv_d2, at(2 * e + far, y))

    def ring(s):
        if s == 0:
            arrived(kbuf.at[0, 1], recv_sib.at[0, 0])
            send(kbuf.at[0, 1], kbuf.at[1, 1], send_ring.at[0, 1], recv_ring.at[1, 1], following)
        elif s < HALF:
            for k in range(2):
                arrived(kbuf.at[s, k], recv_ring.at[s, k])
                if s < HALF - 1:
                    send(kbuf.at[s, k], kbuf.at[s + 1, k], send_ring.at[s, k], recv_ring.at[s + 1, k], following)
                elif k == 0:
                    send(kbuf.at[s, 0], kbuf.at[0, 2], send_ring.at[s, 0], recv_ring.at[0, 0], following)
                send(kbuf.at[s, k], kbuf.at[s, 2 + k], send_sib.at[s, k], recv_sib.at[s, k], (sec, sib))
        else:
            arrived(kbuf.at[0, 2], recv_ring.at[0, 0])
            send(kbuf.at[0, 2], kbuf.at[0, 3], send_sib.at[0, 1], recv_sib.at[0, 1], (sec, sib))

    def spread_rope():
        keep = lax.broadcasted_iota(jnp.int32, (TOKENS, 128), 1) < ROPE

        def one(d, carry):
            for h in range(HEADS):
                pair = qraw[d, :, (h // 2) * 128 : (h // 2 + 1) * 128].astype(f32)
                if h % 2:
                    pair = pltpu.roll(pair, ROPE, 1)
                rel[pl.ds(h, TOKENS, stride=HEADS), :] = jnp.where(keep, pair, 0.0)
            qr[d] = rel[...].astype(bf16)
            return carry

        lax.fori_loop(0, NY, one, 0)

    def attend(s, first):
        if s == 0:
            arrived(kbuf.at[0, 3], recv_sib.at[0, 1])
        else:
            for k in range(2):
                arrived(kbuf.at[s, 2 + k], recv_sib.at[s, k])
        lanes = lax.broadcasted_iota(jnp.int32, (1, 1, 4 * KEYS), 2)
        block, inside = lanes // KEYS, lanes % KEYS
        if s == 0:
            zz = jnp.where(block < 2, z, zplus(HALF))
            cc = jnp.where(block % 2 == 0, c, 1 - c)
        else:
            zz = jnp.where(block < 2, lax.rem(z - onward * s + NZ, NZ), lax.rem(z + onward * s + NZ, NZ))
            cc = jnp.where((block == 0) | (block == 3), c, 1 - c)
        key_pos = ((zz * NY + y) * 2 + cc) * KEYS + inside
        kc = kbuf[s].reshape(4 * KEYS, KW)
        k_lat, k_rope = kc[:, :LATENT], kc[:, LATENT:]
        token_of = lax.broadcasted_iota(jnp.int32, (TOKENS, 1, 1), 0)
        contract = (((1,), (1,)), ((), ()))
        scores = []
        for d in range(NY):
            score = lax.dot_general(ql[d], k_lat, contract, preferred_element_type=f32)
            scores.append(score + lax.dot_general(qr[d], k_rope, contract, preferred_element_type=f32))
        weights = []
        for d in range(NY):
            position = offset_ref[0] + ((z * NY + yplus(d)) * 2 + c) * TOKENS + token_of
            cap = jnp.where(key_pos <= position, jnp.inf, masked_score)
            score = jnp.minimum(scores[d].reshape(TOKENS, HEADS, 4 * KEYS), cap).reshape(ROWS, 4 * KEYS)
            left, right = score[:, :128], score[:, 128:]
            top = jnp.max(jnp.maximum(left, right), axis=1, keepdims=True)
            if first:
                new, alpha = jnp.broadcast_to(top, (ROWS, 128)), None
            else:
                old = m_ref[d]
                new = jnp.maximum(old, top)
                alpha = jnp.exp2((old - new) * scale_log2)
            left = jnp.exp2((left - new) * scale_log2)
            right = jnp.exp2((right - new) * scale_log2)
            m_ref[d] = new
            l_ref[d] = left + right if first else l_ref[d] * alpha + left + right
            weights.append((jnp.concatenate([left.astype(bf16), right.astype(bf16)], axis=1), alpha))
        for d in range(NY):
            weight, alpha = weights[d]
            value = jnp.dot(weight, k_lat, preferred_element_type=f32)
            acc[d] = value if first else acc[d] * jnp.concatenate([alpha] * (LATENT // 128), axis=1) + value

    def spread(half):
        own = xall.at[0, 0, half]
        arrived(own, recv_d2 if half == 0 else recv_d3.at[1, 0])
        if half == 0:
            send(own, xall.at[0, 0, 1], send_d3.at[1, 0], recv_d3.at[1, 0], pair)
        for d in (1, 3, 2) if half == 0 else (1, 3):
            send(own, xall.at[NY - d, 0, half], send_d3.at[half, d], recv_d3.at[half, NY - d], at(z, yplus(d)))
        send(own, xall.at[0, 1, half], send_d3s.at[half, 0], recv_d3s.at[half, 0], (sec, sib))

    def share_rows(half):
        for d in (1, 3, 2):
            got = xall.at[d, 0, half]
            arrived(got, recv_d3.at[half, d])
            if half == 0 and d == 2:
                send(got, xall.at[d, 0, 1], send_d3.at[1, d], recv_d3.at[1, d], pair)
            send(got, xall.at[d, 1, half], send_d3s.at[half, d], recv_d3s.at[half, d], (sec, sib))

    n_rows = HALF * 8

    def experts(half):
        total = None
        for d in range(NY):
            arrived(xall.at[d, 1, half], recv_d3s.at[half, d])
            rows = xall[d, :, half].astype(f32).reshape(2 * n_rows, COLS).astype(bf16)
            term = jnp.dot(rows, wgu[yplus(d)], preferred_element_type=f32)
            total = term if total is None else total + term
        gate, up = total[:, :128], total[:, 128:]
        active = (gate / (1.0 + jnp.exp(-gate)) * up).astype(bf16)
        for d in range(NY):
            piece = jnp.dot(active, wd[yplus(d)], preferred_element_type=f32).reshape(2, HALF, 8, COLS)
            own_sum[half, d] = piece[0]
            csib_send[half, d] = piece[1].astype(bf16)
        send(csib_send.at[half], csib_recv.at[half], send_c0.at[half], recv_c0.at[half], (sec, sib))

    def combine(half):
        arrived(csib_recv.at[half], recv_c0.at[half])
        for d in (1, 3, 2):
            cy_send[half, d - 1] = (own_sum[half, d] + csib_recv[half, d].astype(f32)).astype(bf16)
            send(
                cy_send.at[half, d - 1], cy_recv.at[half, NY - d - 1], send_c1.at[half, d], recv_c1.at[half, NY - d],
                at(z, yplus(d)),
            )

    def give_back(half):
        total = own_sum[half, 0] + csib_recv[half, 0].astype(f32)
        for d in range(1, NY):
            arrived(cy_recv.at[half, d - 1], recv_c1.at[half, d])
            total = total + cy_recv[half, d - 1].astype(f32)
        csum[half] = total.astype(bf16)
        for u in reversed(range(HALF)):
            block = csum.at[half, u]
            if half == 0 and u == 0:
                pltpu.make_async_copy(block, ret.at[z], recv_c2).start()
            else:
                distance = u if half == 0 else -1 - u
                to = at(lax.rem(z + outward * distance + NZ, NZ), y)
                send(block, ret.at[z], send_c2.at[half, u], recv_c2, to)

    def finish():
        arrived(ret, recv_c2)
        pairs = ret[...].astype(f32).reshape(EXPERTS, 2, 8, COLS)
        rows = (pairs[:, 0] + pairs[:, 1]).reshape(8 * EXPERTS, COLS)
        weights = g_recv[...].reshape(NY * TOKENS, 128)[:, : 8 * EXPERTS]
        mixture = jnp.dot(weights, rows, precision=lax.Precision.HIGHEST, preferred_element_type=f32)
        result = mixture.reshape(NY, TOKENS, COLS) + xs_recv[...].astype(f32)
        fin[...] = result.astype(bf16)
        for d in range(NY):
            to = (next_sec, (z * NY + yplus(d)) * 2 + c)
            send(fin.at[d], fin_recv.at[y], send_fin.at[d], recv_fin, to)

    def close(d):
        total = jnp.sum(l_ref[d], axis=1, keepdims=True)
        level = m_ref[d] * scale_log2 + jnp.log2(total)
        return level, acc[d] / total

    def give_out():
        for d in (2, 1, 3):
            level, value = close(d)
            o_send[d - 1] = value.astype(bf16)
            ls_send[d - 1] = jnp.transpose(level)[:8, :]
            to = at(z, yplus(d))
            send(o_send.at[d - 1], o_recv.at[NY - d - 1], send_o.at[0, d], recv_o.at[0, NY - d], to)
            send(ls_send.at[d - 1], ls_recv.at[NY - d - 1], send_o.at[1, d], recv_o.at[1, NY - d], to)

    def merge():
        level, value = close(0)
        levels, values = [level], [value]
        for d in range(1, NY):
            arrived(o_recv.at[d - 1], recv_o.at[0, d])
            arrived(ls_recv.at[d - 1], recv_o.at[1, d])
            levels.append(jnp.transpose(jnp.broadcast_to(ls_recv[d - 1][0:1, :], (128, ROWS))))
        best = functools.reduce(jnp.maximum, levels)
        shares = [jnp.exp2(one - best) for one in levels]
        norm = 1.0 / functools.reduce(jnp.add, shares)
        total = value * jnp.concatenate([shares[0] * norm] * (LATENT // 128), axis=1)
        for d in range(1, NY):
            factor = jnp.concatenate([shares[d] * norm] * (LATENT // 128), axis=1)
            total = total + o_recv[d - 1].astype(f32) * factor
        out_ref[...] = total.astype(bf16)

    def queries():
        for d in (1, 3, 2):
            arrived(ql.at[d], recv_q.at[0, d])
            arrived(qraw.at[d], recv_q.at[1, d])
        locals_[0].wait()
        spread_rope()

    def weights_here():
        for copy in locals_[1:]:
            copy.wait()

    ring(0)
    qraw[0] = qrope_ref[...]
    ring(1)
    ring(2)
    spread(0)
    ring(3)
    spread(1)
    queries()
    attend(1, True)
    ring(4)
    share_rows(0)
    attend(2, False)
    ring(5)
    share_rows(1)
    weights_here()
    experts(0)
    attend(3, False)
    ring(6)
    experts(1)
    combine(0)
    attend(4, False)
    combine(1)
    ring(7)
    attend(5, False)
    give_back(0)
    ring(8)
    attend(6, False)
    attend(7, False)
    give_back(1)
    attend(0, False)
    give_out()
    finish()
    merge()
    arrived(fin_recv, recv_fin)
    for k in range(NY):
        passed_ref[:, k * COLS : (k + 1) * COLS] = fin_recv[k]
    for copy in sends:
        copy.wait_send()


def per_device(
    hidden_rows, expert_ids, gate_weights, w_gate, w_up, w_down, query_latent, query_rope, cache_latent, cache_rope, offsets
):
    vmem = pl.BlockSpec(memory_space=pltpu.VMEM)
    anywhere = pl.BlockSpec(memory_space=pl.ANY)
    dma = pltpu.SemaphoreType.DMA
    passed, attended = pl.pallas_call(
        kernel,
        out_shape=(
            jax.ShapeDtypeStruct((TOKENS, WIDTH), bf16),
            jax.ShapeDtypeStruct((ROWS, LATENT), bf16),
        ),
        in_specs=[
            vmem, vmem, vmem, anywhere, anywhere, anywhere, anywhere, vmem, vmem, vmem,
            pl.BlockSpec(memory_space=pltpu.SMEM),
        ],
        out_specs=(vmem, vmem),
        scratch_shapes=[
            pltpu.VMEM((HALF, 4, KEYS, KW), bf16),
            pltpu.VMEM((NY, ROWS, LATENT), bf16),
            pltpu.VMEM((NY, TOKENS, HEADS * ROPE), bf16),
            pltpu.VMEM((NY, ROWS, 128), bf16),
            pltpu.VMEM((ROWS, 128), f32),
            pltpu.VMEM((NY, ROWS, LATENT), f32),
            pltpu.VMEM((NY, ROWS, 128), f32),
            pltpu.VMEM((NY, ROWS, 128), f32),
            pltpu.VMEM((NY - 1, ROWS, LATENT), bf16),
            pltpu.VMEM((NY - 1, ROWS, LATENT), bf16),
            pltpu.VMEM((NY - 1, 8, ROWS), f32),
            pltpu.VMEM((NY - 1, 8, ROWS), f32),
            pltpu.VMEM((NY, TOKENS, COLS), bf16),
            pltpu.VMEM((NY, TOKENS, COLS), bf16),
            pltpu.VMEM((NY, TOKENS, 128), f32),
            pltpu.VMEM((EXPERTS, 8, COLS), bf16),
            pltpu.VMEM((NY, 2, 2, HALF, 8, COLS), bf16),
            pltpu.VMEM((NY, COLS, 256), bf16),
            pltpu.VMEM((NY, 128, COLS), bf16),
            pltpu.VMEM((2, NY, HALF, 8, COLS), bf16),
            pltpu.VMEM((2, NY, HALF, 8, COLS), bf16),
            pltpu.VMEM((2, NY, HALF, 8, COLS), f32),
            pltpu.VMEM((2, NY - 1, HALF, 8, COLS), bf16),
            pltpu.VMEM((2, NY - 1, HALF, 8, COLS), bf16),
            pltpu.VMEM((2, HALF, 8, COLS), bf16),
            pltpu.VMEM((NZ, 8, COLS), bf16),
            pltpu.VMEM((NY, TOKENS, COLS), bf16),
            pltpu.VMEM((NY, TOKENS, COLS), bf16),
            dma((HALF, 2)), dma((HALF, 2)),
            dma((HALF, 2)), dma((HALF, 2)),
            dma((2, NY)), dma((2, NY)),
            dma((2, NY)), dma((2, NY)),
            dma((2, NY)), dma((2,)),
            dma((HALF,)), dma,
            dma((2, NY)), dma((2, NY)),
            dma((2, NY)), dma((2, NY)),
            dma((2,)), dma((2,)),
            dma((2, NY)), dma((2, NY)),
            dma((2, HALF)), dma,
            dma((NY,)), dma,
            dma((NY, 3)), dma((1,)),
        ],
        compiler_params=pltpu.CompilerParams(
            collective_id=0, has_side_effects=True, vmem_limit_bytes=56 * 1024 * 1024
        ),
        cost_estimate=pl.CostEstimate(flops=6_000_000_000, bytes_accessed=4_000_000, transcendentals=2_000_000),
        name="layer",
    )(
        hidden_rows[0], expert_ids[0], gate_weights[0], w_gate[0], w_up[0], w_down[0],
        query_latent.reshape(ROWS, LATENT), query_rope[0], cache_latent[0], cache_rope[0], offsets,
    )
    return passed[None], attended.reshape(1, TOKENS, HEADS, LATENT)


def solution(mesh):
    rows = P("section", "expert", None)
    heads = P("section", "expert", None, None)
    return jax.shard_map(
        per_device,
        mesh=mesh,
        in_specs=(rows, rows, rows, P("section", None, "expert"), P("section", None, "expert"), rows, heads, rows, rows, rows, P("section")),
        out_specs=(rows, heads),
        check_vma=False,
    )
```

```python
import functools
import math

import jax
import jax.numpy as jnp
from jax import lax
from jax.experimental import pallas as pl
from jax.experimental.pallas import tpu as pltpu
from jax.sharding import PartitionSpec as P

MESH = pl.DeviceIdType.MESH
EXPERTS = 8
NZ, NY = 16, 4
TOKENS, HEADS = 8, 32
ROWS = TOKENS * HEADS
LATENT, ROPE = 512, 64
KEYS = 64
KW = LATENT + 128
WIDTH = 3584
COLS = WIDTH // NY
HALF = NZ // 2
QUART = HALF // 2
PARTS = 4
scale_log2 = 192.0 ** (-0.5) * math.log2(math.e)
masked_score = -1e30
f32, bf16 = jnp.float32, jnp.bfloat16


def kernel(
    x_ref, ids_ref, gate_ref, wg_ref, wu_ref, wd_ref, q_ref, qrope_ref, klat_ref, krope_ref, offset_ref,
    passed_ref, out_ref,
    kbuf, ql, qraw, qr, rel, acc, m_ref, l_ref, o_far, o_far_recv, o_near, o_recv, ls_far, ls_far_recv, ls_near, ls_recv,
    xs, xs_recv, g_recv, packed, hid, xall, wgu, wd, csib_send, csib_recv, own_sum,
    cy_send, cy_recv, csum, pair_recv, ret, fin, fin_recv,
    send_ring, recv_ring, send_sib, recv_sib, send_q, recv_q, send_o, recv_o,
    send_d1, recv_d1, send_d2, recv_d2, send_d3, recv_d3, send_d3s, recv_d3s,
    send_c0, recv_c0, send_c1, recv_c1, send_pair, recv_pair, send_c2, recv_c2, send_fin, recv_fin, sem_w, sem_l,
):
    sec = lax.axis_index("section")
    nsec = lax.axis_size("section")
    me = lax.axis_index("expert")
    c = lax.rem(me, 2)
    y = lax.rem(lax.div(me, 2), NY)
    z = lax.div(me, 2 * NY)
    sib = me + 1 - 2 * c

    def at(zz, yy):
        return (sec, (zz * NY + yy) * 2 + c)

    def zplus(r):
        return lax.rem(z + (r % NZ), NZ)

    def yplus(d):
        return lax.rem(y + (d % NY), NY)

    side = lax.rem(z, 2)
    outward = 2 * side - 1
    pair = at(z - outward, y)
    next_sec = lax.rem(sec + 1, nsec)
    prev_sec = lax.rem(sec + nsec - 1, nsec)
    sends = []

    def send(src, dst, ssem, rsem, device):
        copy = pltpu.make_async_remote_copy(
            src_ref=src, dst_ref=dst, send_sem=ssem, recv_sem=rsem, device_id=device, device_id_type=MESH
        )
        copy.start()
        sends.append(copy)

    def arrived(ref, sem):
        pltpu.make_async_copy(ref, ref, sem).wait()

    barrier = pltpu.get_barrier_semaphore()

    def greet(device):
        pl.semaphore_signal(barrier, inc=1, device_id=device, device_id_type=MESH)

    greet((sec, sib))
    for d in range(1, NY):
        greet(at(z, yplus(d)))
    for r in range(1, NZ):
        greet(at(zplus(r), y))
    for d in range(NY):
        greet((prev_sec, (z * NY + d) * 2 + c))

    locals_ = [pltpu.make_async_copy(q_ref, ql.at[0], sem_l.at[0])]
    for k in range(NY):
        rows = pl.ds(k * COLS, COLS)
        locals_.append(pltpu.make_async_copy(wg_ref.at[rows, :], wgu.at[k, :, pl.ds(0, 128)], sem_w.at[k, 0]))
        locals_.append(pltpu.make_async_copy(wu_ref.at[rows, :], wgu.at[k, :, pl.ds(128, 128)], sem_w.at[k, 1]))
        locals_.append(pltpu.make_async_copy(wd_ref.at[:, rows], wd.at[k], sem_w.at[k, 2]))
    for copy in locals_:
        copy.start()

    kbuf[0, 0, :, :LATENT] = klat_ref[...]
    kbuf[0, 0, :, LATENT:] = jnp.concatenate([krope_ref[...], jnp.zeros((KEYS, 128 - ROPE), bf16)], axis=1)

    lane = lax.broadcasted_iota(jnp.int32, (TOKENS, 128), 1)
    token = lax.broadcasted_iota(jnp.int32, (TOKENS, 128), 0)

    diagonal = lax.broadcasted_iota(jnp.int32, (TOKENS, TOKENS), 0) == lax.broadcasted_iota(jnp.int32, (TOKENS, TOKENS), 1)

    def upright(row):
        return jnp.sum(jnp.where(diagonal, jnp.broadcast_to(row, (TOKENS, TOKENS)), 0.0), axis=1, keepdims=True)

    named_first = upright(ids_ref[0:1, :].astype(f32)).astype(jnp.int32)
    named_second = upright(ids_ref[1:2, :].astype(f32)).astype(jnp.int32)
    share_first, share_second = upright(gate_ref[0:1, :]), upright(gate_ref[1:2, :])

    def slots(lane_e, lane_rank):
        first, second = named_first == lane_e, named_second == lane_e
        hit = jnp.where(first | second, 1, 0)
        rank = jnp.zeros((TOKENS, 128), jnp.int32)
        for t in range(TOKENS - 1):
            rank = rank + jnp.where(token > t, hit[t : t + 1, :], 0)
        share = jnp.where(first, share_first, share_second)
        return jnp.where((hit == 1) & (rank == lane_rank), share, 0.0)

    mine = jnp.where(slots(lane >> 1, lane & 1) != 0.0, 1.0, 0.0)
    pick = jnp.transpose(jnp.concatenate([mine, jnp.zeros((TOKENS, 128), f32)], axis=0))[: 2 * EXPERTS].astype(bf16)
    rows_in = x_ref[...].astype(f32)
    rows_in = jnp.concatenate([rows_in, jnp.zeros_like(rows_in)], axis=0).astype(bf16)
    sorted_rows = jnp.dot(pick, rows_in, preferred_element_type=f32).astype(bf16)
    for k in range(NY):
        xs[k] = sorted_rows[:, k * COLS : (k + 1) * COLS]
    xs_recv[0] = xs[y]
    g_recv[0] = jnp.where(((lane >> 1) & 3) == y, slots(lane >> 3, lane & 1), 0.0)
    to_row = lax.broadcasted_iota(jnp.int32, (8 * EXPERTS, 8 * EXPERTS), 0)
    from_row = lax.broadcasted_iota(jnp.int32, (8 * EXPERTS, 8 * EXPERTS), 1)
    same = ((to_row >> 3) == ((from_row >> 1) & 7)) & ((to_row & 1) == (from_row & 1))
    order = jnp.where(same & (((to_row >> 1) & 3) == (((from_row >> 4) + y) & 3)), 1.0, 0.0).astype(bf16)

    pl.semaphore_wait(barrier, 1 + (NY - 1) + (NZ - 1) + NY)

    for d in range(1, NY):
        to = at(z, yplus(d))
        send(xs.at[yplus(d)], xs_recv.at[NY - d], send_d1.at[0, d], recv_d1.at[0], to)
        send(g_recv.at[0], g_recv.at[NY - d], send_d1.at[1, d], recv_d1.at[1], to)
    onward = 1 - 2 * c
    following = at(lax.rem(z + onward + NZ, NZ), y)
    send(kbuf.at[0, 0], kbuf.at[1, 0], send_ring.at[0, 0], recv_ring.at[1, 0], following)
    send(kbuf.at[0, 0], kbuf.at[0, 1], send_sib.at[0, 0], recv_sib.at[0, 0], (sec, sib))
    for d in (1, 3):
        to = at(z, yplus(d))
        send(q_ref, ql.at[NY - d], send_q.at[0, d], recv_q.at[0, NY - d], to)
        send(qrope_ref, qraw.at[NY - d], send_q.at[1, d], recv_q.at[1, NY - d], to)

    def dispatch():
        arrived(xs_recv.at[pl.ds(1, NY - 1)], recv_d1.at[0])
        rows = jnp.dot(order, xs_recv[...].reshape(8 * EXPERTS, COLS), preferred_element_type=f32)
        packed[...] = rows.reshape(EXPERTS, 8, COLS).astype(bf16)
        pltpu.make_async_copy(packed.at[lax.div(z, 2)], xall.at[0, 0, 0, 0], recv_d2.at[0]).start()
        for i in (1, 7, 2, 6, 3, 5, 4):
            e = lax.rem(lax.div(z, 2) + i, EXPERTS)
            delta = 2 * i - side
            far = lax.div(delta, HALF)
            u = delta + far * (NZ - 1 - 2 * delta)
            part = lax.div(u, QUART)
            slot = xall.at[0, 0, part, lax.rem(u, QUART)]
            send(packed.at[e], slot, send_d2.at[i], recv_d2.at[part], at(2 * e + far, y))

    def gates():
        return g_recv[...].reshape(NY * TOKENS, 128)[:, : 8 * EXPERTS]

    def keep_rows():
        arrived(g_recv.at[pl.ds(1, NY - 1)], recv_d1.at[1])
        named = jnp.where(gates() != 0.0, 0.5, 0.0).astype(bf16)
        rows = packed[...].astype(f32).reshape(8 * EXPERTS, COLS).astype(bf16)
        hid[...] = jnp.dot(named, rows, preferred_element_type=f32)

    def ring(s):
        if s == 0:
            arrived(kbuf.at[0, 1], recv_sib.at[0, 0])
            send(kbuf.at[0, 1], kbuf.at[1, 1], send_ring.at[0, 1], recv_ring.at[1, 1], following)
        elif s < HALF:
            for k in range(2):
                arrived(kbuf.at[s, k], recv_ring.at[s, k])
                if s < HALF - 1:
                    send(kbuf.at[s, k], kbuf.at[s + 1, k], send_ring.at[s, k], recv_ring.at[s + 1, k], following)
                elif k == 0:
                    send(kbuf.at[s, 0], kbuf.at[0, 2], send_ring.at[s, 0], recv_ring.at[0, 0], following)
                send(kbuf.at[s, k], kbuf.at[s, 2 + k], send_sib.at[s, k], recv_sib.at[s, k], (sec, sib))
        else:
            arrived(kbuf.at[0, 2], recv_ring.at[0, 0])
            send(kbuf.at[0, 2], kbuf.at[0, 3], send_sib.at[0, 1], recv_sib.at[0, 1], (sec, sib))

    def spread_rope():
        keep = lax.broadcasted_iota(jnp.int32, (TOKENS, 128), 1) < ROPE

        def one(d, carry):
            for h in range(HEADS):
                pair = qraw[d, :, (h // 2) * 128 : (h // 2 + 1) * 128].astype(f32)
                if h % 2:
                    pair = pltpu.roll(pair, ROPE, 1)
                rel[pl.ds(h, TOKENS, stride=HEADS), :] = jnp.where(keep, pair, 0.0)
            qr[d] = rel[...].astype(bf16)
            return carry

        lax.fori_loop(0, NY, one, 0)

    def attend(s, first):
        if s == 0:
            arrived(kbuf.at[0, 3], recv_sib.at[0, 1])
        else:
            for k in range(2):
                arrived(kbuf.at[s, 2 + k], recv_sib.at[s, k])
        lanes = lax.broadcasted_iota(jnp.int32, (1, 1, 4 * KEYS), 2)
        block, inside = lanes // KEYS, lanes % KEYS
        if s == 0:
            zz = jnp.where(block < 2, z, zplus(HALF))
            cc = jnp.where(block % 2 == 0, c, 1 - c)
        else:
            zz = jnp.where(block < 2, lax.rem(z - onward * s + NZ, NZ), lax.rem(z + onward * s + NZ, NZ))
            cc = jnp.where((block == 0) | (block == 3), c, 1 - c)
        key_pos = ((zz * NY + y) * 2 + cc) * KEYS + inside
        kc = kbuf[s].reshape(4 * KEYS, KW)
        k_lat, k_rope = kc[:, :LATENT], kc[:, LATENT:]
        token_of = lax.broadcasted_iota(jnp.int32, (TOKENS, 1, 1), 0)
        contract = (((1,), (1,)), ((), ()))
        scores = []
        for d in range(NY):
            score = lax.dot_general(ql[d], k_lat, contract, preferred_element_type=f32)
            scores.append(score + lax.dot_general(qr[d], k_rope, contract, preferred_element_type=f32))
        weights = []
        for d in range(NY):
            position = offset_ref[0] + ((z * NY + yplus(d)) * 2 + c) * TOKENS + token_of
            cap = jnp.where(key_pos <= position, jnp.inf, masked_score)
            score = jnp.minimum(scores[d].reshape(TOKENS, HEADS, 4 * KEYS), cap).reshape(ROWS, 4 * KEYS)
            left, right = score[:, :128], score[:, 128:]
            top = jnp.max(jnp.maximum(left, right), axis=1, keepdims=True)
            if first:
                new, alpha = jnp.broadcast_to(top, (ROWS, 128)), None
            else:
                old = m_ref[d]
                new = jnp.maximum(old, top)
                alpha = jnp.exp2((old - new) * scale_log2)
            left = jnp.exp2((left - new) * scale_log2)
            right = jnp.exp2((right - new) * scale_log2)
            m_ref[d] = new
            l_ref[d] = left + right if first else l_ref[d] * alpha + left + right
            weights.append((jnp.concatenate([left.astype(bf16), right.astype(bf16)], axis=1), alpha))
        for d in range(NY):
            weight, alpha = weights[d]
            value = jnp.dot(weight, k_lat, preferred_element_type=f32)
            acc[d] = value if first else acc[d] * jnp.concatenate([alpha] * (LATENT // 128), axis=1) + value

    def spread(p):
        own = xall.at[0, 0, p]
        arrived(own, recv_d2.at[p] if p < 2 else recv_d3.at[p, 0])
        if p < 2:
            send(own, xall.at[0, 0, p + 2], send_d3.at[p + 2, 0], recv_d3.at[p + 2, 0], pair)
        for d in (2, 1, 3) if p < 2 else (1, 3):
            send(own, xall.at[NY - d, 0, p], send_d3.at[p, d], recv_d3.at[p, NY - d], at(z, yplus(d)))
        send(own, xall.at[0, 1, p], send_d3s.at[p, 0], recv_d3s.at[p, 0], (sec, sib))

    def share_rows(p):
        for d in (1, 3, 2):
            arrived(xall.at[d, 0, p], recv_d3.at[p, d])
            if d == 2 and p < 2:
                send(xall.at[2, 0, p], xall.at[2, 0, p + 2], send_d3.at[p + 2, 2], recv_d3.at[p + 2, 2], pair)
            send(xall.at[d, 0, p], xall.at[d, 1, p], send_d3s.at[p, d], recv_d3s.at[p, d], (sec, sib))

    n_rows = QUART * 8

    def experts(p):
        total = None
        for d in (0, 1, 3, 2):
            arrived(xall.at[d, 1, p], recv_d3s.at[p, d])
            rows = xall[d, :, p].astype(f32).reshape(2 * n_rows, COLS).astype(bf16)
            term = jnp.dot(rows, wgu[yplus(d)], preferred_element_type=f32)
            total = term if total is None else total + term
        gate, up = total[:, :128], total[:, 128:]
        active = (gate / (1.0 + jnp.exp(-gate)) * up).astype(bf16)
        for d in range(NY):
            piece = jnp.dot(active, wd[yplus(d)], preferred_element_type=f32).reshape(2, QUART, 8, COLS)
            own_sum[p, d] = piece[0]
            csib_send[p, d] = piece[1].astype(bf16)
        send(csib_send.at[p], csib_recv.at[p], send_c0.at[p], recv_c0.at[p], (sec, sib))

    def chunk(p, d):
        return own_sum[p, d] + csib_recv[p, d].astype(f32)

    def combine(p):
        arrived(csib_recv.at[p], recv_c0.at[p])
        if p >= 2:
            cy_send[p, 1] = chunk(p, 2).astype(bf16)
            send(cy_send.at[p, 1], pair_recv.at[0, p - 2], send_pair.at[0, p - 2], recv_pair.at[0, p - 2], pair)
        for d in (1, 3):
            cy_send[p, d - 1] = chunk(p, d).astype(bf16)
            send(
                cy_send.at[p, d - 1], cy_recv.at[p, NY - d - 1], send_c1.at[p, d], recv_c1.at[p, NY - d], at(z, yplus(d))
            )

    def combine_far(p):
        arrived(pair_recv.at[0, p], recv_pair.at[0, p])
        cy_send[p, 1] = (chunk(p, 2) + pair_recv[0, p].astype(f32)).astype(bf16)
        send(cy_send.at[p, 1], cy_recv.at[p, 1], send_c1.at[p, 2], recv_c1.at[p, 2], at(z, yplus(2)))

    def give_back(p):
        total = chunk(p, 0)
        for d in (1, 3, 2) if p < 2 else (1, 3):
            arrived(cy_recv.at[p, d - 1], recv_c1.at[p, d])
            total = total + cy_recv[p, d - 1].astype(f32)
        if p >= 2:
            csum[p] = total.astype(bf16)
            send(csum.at[p], pair_recv.at[1, p - 2], send_pair.at[1, p - 2], recv_pair.at[1, p - 2], pair)
            return
        arrived(pair_recv.at[1, p], recv_pair.at[1, p])
        csum[p] = (total + pair_recv[1, p].astype(f32)).astype(bf16)
        for k in reversed(range(QUART)):
            u = k + QUART * p
            home = ret.at[lax.div(z, 2)]
            if u == 0:
                pltpu.make_async_copy(csum.at[p, k], home, recv_c2).start()
            else:
                to = at(lax.rem(z + outward * u + NZ, NZ), y)
                send(csum.at[p, k], home, send_c2.at[p, k], recv_c2, to)

    def finish():
        arrived(ret, recv_c2)
        rows = ret[...].astype(f32).reshape(8 * EXPERTS, COLS).astype(bf16)
        weights = gates()
        high = weights.astype(bf16)
        low = (weights - high.astype(f32)).astype(bf16)
        mixture = jnp.dot(high, rows, preferred_element_type=f32) + jnp.dot(low, rows, preferred_element_type=f32)
        result = (hid[...] + mixture).reshape(NY, TOKENS, COLS)
        fin[...] = result.astype(bf16)
        for d in range(NY):
            to = (next_sec, (z * NY + yplus(d)) * 2 + c)
            send(fin.at[d], fin_recv.at[y], send_fin.at[d], recv_fin, to)

    def close(d):
        total = jnp.sum(l_ref[d], axis=1, keepdims=True)
        level = m_ref[d] * scale_log2 + jnp.log2(total)
        return level, acc[d] * (1.0 / total)

    def wide(factor):
        return jnp.concatenate([factor] * (LATENT // 128), axis=1)

    def column(ref, start, size):
        return jnp.transpose(jnp.broadcast_to(ref[0:1, start : start + size], (128, size)))

    half_rows = ROWS // 2

    def give_out_far():
        level, value = close(2)
        o_far[...] = value.astype(bf16).reshape(2, half_rows, LATENT)
        ls_far[...] = jnp.transpose(level)[:8, :]
        for q in range(2):
            to = at(z, yplus(1 + 2 * q))
            send(o_far.at[q], o_far_recv.at[q], send_o.at[q, 0], recv_o.at[q, 0], to)
            send(ls_far, ls_far_recv.at[q], send_o.at[q, 1], recv_o.at[q, 1], to)
        for q in range(2):
            to = at(z, yplus(1 + 2 * q))
            level, value = close(1 + 2 * q)
            m_ref[1 + 2 * q] = level
            acc[1 + 2 * q] = value
            rest = slice((1 - q) * half_rows, (2 - q) * half_rows)
            o_near[q, 1 - q] = value[rest].astype(bf16)
            send(o_near.at[q, 1 - q], o_recv.at[q, 1 - q], send_o.at[q, 2], recv_o.at[q, 2], to)

    def give_out_near():
        for q in range(2):
            to = at(z, yplus(1 + 2 * q))
            arrived(o_far_recv.at[q], recv_o.at[q, 0])
            arrived(ls_far_recv.at[q], recv_o.at[q, 1])
            rows = slice(q * half_rows, (q + 1) * half_rows)
            here, there = m_ref[1 + 2 * q, rows], column(ls_far_recv.at[q], q * half_rows, half_rows)
            best = jnp.maximum(here, there)
            here, there = jnp.exp2(here - best), jnp.exp2(there - best)
            norm = 1.0 / (here + there)
            value = acc[1 + 2 * q, rows] * wide(here * norm) + o_far_recv[q].astype(f32) * wide(there * norm)
            o_near[q, q] = value.astype(bf16)
            m_ref[1 + 2 * q, rows] = best + jnp.log2(here + there)
            ls_near[q] = jnp.transpose(m_ref[1 + 2 * q])[:8, :]
            send(o_near.at[q, q], o_recv.at[q, q], send_o.at[q, 3], recv_o.at[q, 3], to)
            send(ls_near.at[q], ls_recv.at[q], send_o.at[q, 4], recv_o.at[q, 4], to)

    def merge():
        level, value = close(0)
        levels, values = [level], [value]
        for q in range(2):
            arrived(o_recv.at[q, 1 - q], recv_o.at[q, 2])
            arrived(o_recv.at[q, q], recv_o.at[q, 3])
            arrived(ls_recv.at[q], recv_o.at[q, 4])
            levels.append(column(ls_recv.at[q], 0, ROWS))
            values.append(o_recv[q].reshape(ROWS, LATENT).astype(f32))
        best = functools.reduce(jnp.maximum, levels)
        shares = [jnp.exp2(one - best) for one in levels]
        norm = 1.0 / functools.reduce(jnp.add, shares)
        out_ref[...] = sum(one * wide(share * norm) for one, share in zip(values, shares)).astype(bf16)

    def queries_on():
        for d in (1, 3):
            q = d // 2
            rows = pl.ds(q * half_rows, half_rows)
            to = at(z, yplus(NY - d))
            arrived(ql.at[d], recv_q.at[0, d])
            send(ql.at[d, rows], ql.at[2, rows], send_q.at[2, q], recv_q.at[2, q], to)
            arrived(qraw.at[d], recv_q.at[1, d])
            if q == 0:
                send(qraw.at[d], qraw.at[2], send_q.at[1, 2], recv_q.at[1, 2], to)

    def queries():
        for q in range(2):
            arrived(ql.at[2, pl.ds(q * half_rows, half_rows)], recv_q.at[2, q])
        arrived(qraw.at[2], recv_q.at[1, 2])
        locals_[0].wait()
        spread_rope()

    def weights_here():
        for copy in locals_[1:]:
            copy.wait()

    dispatch()
    ring(0)
    qraw[0] = qrope_ref[...]
    ring(1)
    spread(0)
    keep_rows()
    queries_on()
    ring(2)
    spread(2)
    spread(1)
    ring(3)
    share_rows(0)
    spread(3)
    share_rows(2)
    weights_here()
    ring(4)
    experts(0)
    share_rows(1)
    experts(2)
    queries()
    ring(5)
    share_rows(3)
    combine(2)
    experts(1)
    combine(0)
    attend(1, True)
    experts(3)
    ring(6)
    attend(2, False)
    combine(3)
    combine(1)
    combine_far(0)
    give_back(2)
    ring(7)
    attend(3, False)
    combine_far(1)
    attend(4, False)
    give_back(3)
    ring(8)
    attend(5, False)
    give_back(0)
    attend(6, False)
    attend(7, False)
    give_back(1)
    attend(0, False)
    give_out_far()
    give_out_near()
    finish()
    merge()
    arrived(fin_recv, recv_fin)
    for k in range(NY):
        passed_ref[:, k * COLS : (k + 1) * COLS] = fin_recv[k]
    for copy in sends:
        copy.wait_send()


def per_device(
    hidden_rows, expert_ids, gate_weights, w_gate, w_up, w_down, query_latent, query_rope, cache_latent, cache_rope, offsets
):
    vmem = pl.BlockSpec(memory_space=pltpu.VMEM)
    anywhere = pl.BlockSpec(memory_space=pl.ANY)
    dma = pltpu.SemaphoreType.DMA
    passed, attended = pl.pallas_call(
        kernel,
        out_shape=(
            jax.ShapeDtypeStruct((TOKENS, WIDTH), bf16),
            jax.ShapeDtypeStruct((ROWS, LATENT), bf16),
        ),
        in_specs=[
            vmem, vmem, vmem, anywhere, anywhere, anywhere, anywhere, vmem, vmem, vmem,
            pl.BlockSpec(memory_space=pltpu.SMEM),
        ],
        out_specs=(vmem, vmem),
        scratch_shapes=[
            pltpu.VMEM((HALF, 4, KEYS, KW), bf16),
            pltpu.VMEM((NY, ROWS, LATENT), bf16),
            pltpu.VMEM((NY, TOKENS, HEADS * ROPE), bf16),
            pltpu.VMEM((NY, ROWS, 128), bf16),
            pltpu.VMEM((ROWS, 128), f32),
            pltpu.VMEM((NY, ROWS, LATENT), f32),
            pltpu.VMEM((NY, ROWS, 128), f32),
            pltpu.VMEM((NY, ROWS, 128), f32),
            pltpu.VMEM((2, ROWS // 2, LATENT), bf16),
            pltpu.VMEM((2, ROWS // 2, LATENT), bf16),
            pltpu.VMEM((2, 2, ROWS // 2, LATENT), bf16),
            pltpu.VMEM((2, 2, ROWS // 2, LATENT), bf16),
            pltpu.VMEM((8, ROWS), f32),
            pltpu.VMEM((2, 8, ROWS), f32),
            pltpu.VMEM((2, 8, ROWS), f32),
            pltpu.VMEM((2, 8, ROWS), f32),
            pltpu.VMEM((NY, 2 * EXPERTS, COLS), bf16),
            pltpu.VMEM((NY, 2 * EXPERTS, COLS), bf16),
            pltpu.VMEM((NY, TOKENS, 128), f32),
            pltpu.VMEM((EXPERTS, 8, COLS), bf16),
            pltpu.VMEM((NY * TOKENS, COLS), f32),
            pltpu.VMEM((NY, 2, PARTS, QUART, 8, COLS), bf16),
            pltpu.VMEM((NY, COLS, 256), bf16),
            pltpu.VMEM((NY, 128, COLS), bf16),
            pltpu.VMEM((PARTS, NY, QUART, 8, COLS), bf16),
            pltpu.VMEM((PARTS, NY, QUART, 8, COLS), bf16),
            pltpu.VMEM((PARTS, NY, QUART, 8, COLS), f32),
            pltpu.VMEM((PARTS, NY - 1, QUART, 8, COLS), bf16),
            pltpu.VMEM((PARTS, NY - 1, QUART, 8, COLS), bf16),
            pltpu.VMEM((PARTS, QUART, 8, COLS), bf16),
            pltpu.VMEM((2, 2, QUART, 8, COLS), bf16),
            pltpu.VMEM((EXPERTS, 8, COLS), bf16),
            pltpu.VMEM((NY, TOKENS, COLS), bf16),
            pltpu.VMEM((NY, TOKENS, COLS), bf16),
            dma((HALF, 2)), dma((HALF, 2)),
            dma((HALF, 2)), dma((HALF, 2)),
            dma((3, NY)), dma((3, NY)),
            dma((2, 5)), dma((2, 5)),
            dma((2, NY)), dma((2,)),
            dma((HALF,)), dma((2,)),
            dma((PARTS, NY)), dma((PARTS, NY)),
            dma((PARTS, NY)), dma((PARTS, NY)),
            dma((PARTS,)), dma((PARTS,)),
            dma((PARTS, NY)), dma((PARTS, NY)),
            dma((2, 2)), dma((2, 2)),
            dma((2, QUART)), dma,
            dma((NY,)), dma,
            dma((NY, 3)), dma((1,)),
        ],
        compiler_params=pltpu.CompilerParams(
            collective_id=0, has_side_effects=True, vmem_limit_bytes=56 * 1024 * 1024
        ),
        cost_estimate=pl.CostEstimate(flops=6_000_000_000, bytes_accessed=4_000_000, transcendentals=2_000_000),
        name="layer",
    )(
        hidden_rows[0], expert_ids[0].T, gate_weights[0].T, w_gate[0], w_up[0], w_down[0],
        query_latent.reshape(ROWS, LATENT), query_rope[0], cache_latent[0], cache_rope[0], offsets,
    )
    return passed[None], attended.reshape(1, TOKENS, HEADS, LATENT)


def solution(mesh):
    rows = P("section", "expert", None)
    heads = P("section", "expert", None, None)
    return jax.shard_map(
        per_device,
        mesh=mesh,
        in_specs=(rows, rows, rows, P("section", None, "expert"), P("section", None, "expert"), rows, heads, rows, rows, rows, P("section")),
        out_specs=(rows, heads),
        check_vma=False,
    )
```

```python
import functools
import math

import jax
import jax.numpy as jnp
from jax import lax
from jax.experimental import pallas as pl
from jax.experimental.pallas import tpu as pltpu
from jax.sharding import PartitionSpec as P

MESH = pl.DeviceIdType.MESH
EXPERTS = 8
NZ, NY = 16, 4
TOKENS, HEADS = 8, 32
ROWS = TOKENS * HEADS
LATENT, ROPE = 512, 64
KEYS = 64
KW = LATENT + 128
WIDTH = 3584
COLS = WIDTH // NY
HALF = NZ // 2
QUART = HALF // 2
PARTS = 4
scale_log2 = 192.0 ** (-0.5) * math.log2(math.e)
masked_score = -1e30
f32, bf16 = jnp.float32, jnp.bfloat16


def kernel(
    x_hbm, ids_hbm, gate_hbm, wg_ref, wu_ref, wd_ref, q_ref, qrope_hbm, klat_hbm, krope_hbm, offset_ref,
    passed_ref, out_ref,
    kbuf, ql, qraw, qr, rel, acc, m_ref, l_ref, o_far, o_far_recv, o_near, o_recv, ls_far, ls_far_recv, ls_near, ls_recv,
    xs, xs_recv, g_recv, packed, hid, xall, wgu, wd, csib_send, csib_recv, own_sum,
    cy_send, cy_recv, csum, pair_recv, ret, fin, fin_recv,
    send_ring, recv_ring, send_sib, recv_sib, send_q, recv_q, send_o, recv_o,
    send_d1, recv_d1, send_d2, recv_d2, send_d3, recv_d3, send_d3s, recv_d3s,
    send_c0, recv_c0, send_c1, recv_c1, send_pair, recv_pair, send_c2, recv_c2, send_fin, recv_fin, sem_w, sem_l,
    x_ref, ids_ref, gate_ref, qrope_ref, klat_ref, krope_ref, sem_in,
):
    sec = lax.axis_index("section")
    nsec = lax.axis_size("section")
    me = lax.axis_index("expert")
    c = lax.rem(me, 2)
    y = lax.rem(lax.div(me, 2), NY)
    z = lax.div(me, 2 * NY)
    sib = me + 1 - 2 * c

    def at(zz, yy):
        return (sec, (zz * NY + yy) * 2 + c)

    def zplus(r):
        return lax.rem(z + (r % NZ), NZ)

    def yplus(d):
        return lax.rem(y + (d % NY), NY)

    side = lax.rem(z, 2)
    outward = 2 * side - 1
    pair = at(z - outward, y)
    next_sec = lax.rem(sec + 1, nsec)
    prev_sec = lax.rem(sec + nsec - 1, nsec)
    sends = []

    def send(src, dst, ssem, rsem, device):
        copy = pltpu.make_async_remote_copy(
            src_ref=src, dst_ref=dst, send_sem=ssem, recv_sem=rsem, device_id=device, device_id_type=MESH
        )
        copy.start()
        sends.append(copy)

    def arrived(ref, sem):
        pltpu.make_async_copy(ref, ref, sem).wait()

    barrier = pltpu.get_barrier_semaphore()

    def greet(device):
        pl.semaphore_signal(barrier, inc=1, device_id=device, device_id_type=MESH)

    greet((sec, sib))
    for d in range(1, NY):
        greet(at(z, yplus(d)))
    for r in range(1, NZ):
        greet(at(zplus(r), y))
    for d in range(NY):
        greet((prev_sec, (z * NY + d) * 2 + c))

    pairs = [
        (ids_hbm, ids_ref), (gate_hbm, gate_ref), (x_hbm, x_ref), (klat_hbm, klat_ref), (krope_hbm, krope_ref),
        (qrope_hbm, qrope_ref),
    ]
    small = [pltpu.make_async_copy(src, dst, sem_in.at[k]) for k, (src, dst) in enumerate(pairs)]
    for copy in small:
        copy.start()
    locals_ = [pltpu.make_async_copy(q_ref, ql.at[0], sem_l.at[0])]
    for k in range(NY):
        rows = pl.ds(k * COLS, COLS)
        locals_.append(pltpu.make_async_copy(wg_ref.at[rows, :], wgu.at[k, :, pl.ds(0, 128)], sem_w.at[k, 0]))
        locals_.append(pltpu.make_async_copy(wu_ref.at[rows, :], wgu.at[k, :, pl.ds(128, 128)], sem_w.at[k, 1]))
        locals_.append(pltpu.make_async_copy(wd_ref.at[:, rows], wd.at[k], sem_w.at[k, 2]))
    for copy in locals_:
        copy.start()

    for copy in small:
        copy.wait()
    kbuf[0, 0, :, :LATENT] = klat_ref[...]
    kbuf[0, 0, :, LATENT:] = jnp.concatenate([krope_ref[...], jnp.zeros((KEYS, 128 - ROPE), bf16)], axis=1)

    lane = lax.broadcasted_iota(jnp.int32, (TOKENS, 128), 1)
    token = lax.broadcasted_iota(jnp.int32, (TOKENS, 128), 0)

    diagonal = lax.broadcasted_iota(jnp.int32, (TOKENS, TOKENS), 0) == lax.broadcasted_iota(jnp.int32, (TOKENS, TOKENS), 1)

    def upright(row):
        return jnp.sum(jnp.where(diagonal, jnp.broadcast_to(row, (TOKENS, TOKENS)), 0.0), axis=1, keepdims=True)

    named_first = upright(ids_ref[0:1, :].astype(f32)).astype(jnp.int32)
    named_second = upright(ids_ref[1:2, :].astype(f32)).astype(jnp.int32)
    share_first, share_second = upright(gate_ref[0:1, :]), upright(gate_ref[1:2, :])

    def slots(lane_e, lane_rank):
        first, second = named_first == lane_e, named_second == lane_e
        hit = jnp.where(first | second, 1, 0)
        rank = jnp.zeros((TOKENS, 128), jnp.int32)
        for t in range(TOKENS - 1):
            rank = rank + jnp.where(token > t, hit[t : t + 1, :], 0)
        share = jnp.where(first, share_first, share_second)
        return jnp.where((hit == 1) & (rank == lane_rank), share, 0.0)

    mine = jnp.where(slots(lane >> 1, lane & 1) != 0.0, 1.0, 0.0)
    pick = jnp.transpose(jnp.concatenate([mine, jnp.zeros((TOKENS, 128), f32)], axis=0))[: 2 * EXPERTS].astype(bf16)
    rows_in = x_ref[...].astype(f32)
    rows_in = jnp.concatenate([rows_in, jnp.zeros_like(rows_in)], axis=0).astype(bf16)
    sorted_rows = jnp.dot(pick, rows_in, preferred_element_type=f32).astype(bf16)
    for k in range(NY):
        xs[k] = sorted_rows[:, k * COLS : (k + 1) * COLS]
    xs_recv[0] = xs[y]
    g_recv[0] = jnp.where(((lane >> 1) & 3) == y, slots(lane >> 3, lane & 1), 0.0)
    to_row = lax.broadcasted_iota(jnp.int32, (8 * EXPERTS, 8 * EXPERTS), 0)
    from_row = lax.broadcasted_iota(jnp.int32, (8 * EXPERTS, 8 * EXPERTS), 1)
    same = ((to_row >> 3) == ((from_row >> 1) & 7)) & ((to_row & 1) == (from_row & 1))
    order = jnp.where(same & (((to_row >> 1) & 3) == (((from_row >> 4) + y) & 3)), 1.0, 0.0).astype(bf16)

    pl.semaphore_wait(barrier, 1 + (NY - 1) + (NZ - 1) + NY)

    for d in range(1, NY):
        to = at(z, yplus(d))
        send(xs.at[yplus(d)], xs_recv.at[NY - d], send_d1.at[0, d], recv_d1.at[0], to)
        send(g_recv.at[0], g_recv.at[NY - d], send_d1.at[1, d], recv_d1.at[1], to)
    onward = 1 - 2 * c
    following = at(lax.rem(z + onward + NZ, NZ), y)
    send(kbuf.at[0, 0], kbuf.at[1, 0], send_ring.at[0, 0], recv_ring.at[1, 0], following)
    send(kbuf.at[0, 0], kbuf.at[0, 1], send_sib.at[0, 0], recv_sib.at[0, 0], (sec, sib))
    for d in (1, 3):
        to = at(z, yplus(d))
        send(q_ref, ql.at[NY - d], send_q.at[0, d], recv_q.at[0, NY - d], to)
        send(qrope_ref, qraw.at[NY - d], send_q.at[1, d], recv_q.at[1, NY - d], to)

    def dispatch():
        arrived(xs_recv.at[pl.ds(1, NY - 1)], recv_d1.at[0])
        rows = jnp.dot(order, xs_recv[...].reshape(8 * EXPERTS, COLS), preferred_element_type=f32)
        packed[...] = rows.reshape(EXPERTS, 8, COLS).astype(bf16)
        pltpu.make_async_copy(packed.at[lax.div(z, 2)], xall.at[0, 0, 0, 0], recv_d2.at[0]).start()
        for i in (1, 7, 2, 6, 3, 5, 4):
            e = lax.rem(lax.div(z, 2) + i, EXPERTS)
            delta = 2 * i - side
            far = lax.div(delta, HALF)
            u = delta + far * (NZ - 1 - 2 * delta)
            part = lax.div(u, QUART)
            slot = xall.at[0, 0, part, lax.rem(u, QUART)]
            send(packed.at[e], slot, send_d2.at[i], recv_d2.at[part], at(2 * e + far, y))

    def gates():
        return g_recv[...].reshape(NY * TOKENS, 128)[:, : 8 * EXPERTS]

    def keep_rows():
        arrived(g_recv.at[pl.ds(1, NY - 1)], recv_d1.at[1])
        named = jnp.where(gates() != 0.0, 0.5, 0.0).astype(bf16)
        rows = packed[...].astype(f32).reshape(8 * EXPERTS, COLS).astype(bf16)
        hid[...] = jnp.dot(named, rows, preferred_element_type=f32)

    def ring(s):
        if s == 0:
            arrived(kbuf.at[0, 1], recv_sib.at[0, 0])
            send(kbuf.at[0, 1], kbuf.at[1, 1], send_ring.at[0, 1], recv_ring.at[1, 1], following)
        elif s < HALF:
            for k in range(2):
                arrived(kbuf.at[s, k], recv_ring.at[s, k])
                if s < HALF - 1:
                    send(kbuf.at[s, k], kbuf.at[s + 1, k], send_ring.at[s, k], recv_ring.at[s + 1, k], following)
                elif k == 0:
                    send(kbuf.at[s, 0], kbuf.at[0, 2], send_ring.at[s, 0], recv_ring.at[0, 0], following)
                send(kbuf.at[s, k], kbuf.at[s, 2 + k], send_sib.at[s, k], recv_sib.at[s, k], (sec, sib))
        else:
            arrived(kbuf.at[0, 2], recv_ring.at[0, 0])
            send(kbuf.at[0, 2], kbuf.at[0, 3], send_sib.at[0, 1], recv_sib.at[0, 1], (sec, sib))

    def spread_rope():
        keep = lax.broadcasted_iota(jnp.int32, (TOKENS, 128), 1) < ROPE

        def one(d, carry):
            for h in range(HEADS):
                pair = qraw[d, :, (h // 2) * 128 : (h // 2 + 1) * 128].astype(f32)
                if h % 2:
                    pair = pltpu.roll(pair, ROPE, 1)
                rel[pl.ds(h, TOKENS, stride=HEADS), :] = jnp.where(keep, pair, 0.0)
            qr[d] = rel[...].astype(bf16)
            return carry

        lax.fori_loop(0, NY, one, 0)

    def attend(s, first):
        if s == 0:
            arrived(kbuf.at[0, 3], recv_sib.at[0, 1])
        else:
            for k in range(2):
                arrived(kbuf.at[s, 2 + k], recv_sib.at[s, k])
        lanes = lax.broadcasted_iota(jnp.int32, (1, 1, 4 * KEYS), 2)
        block, inside = lanes // KEYS, lanes % KEYS
        if s == 0:
            zz = jnp.where(block < 2, z, zplus(HALF))
            cc = jnp.where(block % 2 == 0, c, 1 - c)
        else:
            zz = jnp.where(block < 2, lax.rem(z - onward * s + NZ, NZ), lax.rem(z + onward * s + NZ, NZ))
            cc = jnp.where((block == 0) | (block == 3), c, 1 - c)
        key_pos = ((zz * NY + y) * 2 + cc) * KEYS + inside
        kc = kbuf[s].reshape(4 * KEYS, KW)
        k_lat, k_rope = kc[:, :LATENT], kc[:, LATENT:]
        token_of = lax.broadcasted_iota(jnp.int32, (TOKENS, 1, 1), 0)
        contract = (((1,), (1,)), ((), ()))
        scores = []
        for d in range(NY):
            score = lax.dot_general(ql[d], k_lat, contract, preferred_element_type=f32)
            scores.append(score + lax.dot_general(qr[d], k_rope, contract, preferred_element_type=f32))
        weights = []
        for d in range(NY):
            position = offset_ref[0] + ((z * NY + yplus(d)) * 2 + c) * TOKENS + token_of
            cap = jnp.where(key_pos <= position, jnp.inf, masked_score)
            score = jnp.minimum(scores[d].reshape(TOKENS, HEADS, 4 * KEYS), cap).reshape(ROWS, 4 * KEYS)
            left, right = score[:, :128], score[:, 128:]
            top = jnp.max(jnp.maximum(left, right), axis=1, keepdims=True)
            if first:
                new, alpha = jnp.broadcast_to(top, (ROWS, 128)), None
            else:
                old = m_ref[d]
                new = jnp.maximum(old, top)
                alpha = jnp.exp2((old - new) * scale_log2)
            left = jnp.exp2((left - new) * scale_log2)
            right = jnp.exp2((right - new) * scale_log2)
            m_ref[d] = new
            l_ref[d] = left + right if first else l_ref[d] * alpha + left + right
            weights.append((jnp.concatenate([left.astype(bf16), right.astype(bf16)], axis=1), alpha))
        for d in range(NY):
            weight, alpha = weights[d]
            value = jnp.dot(weight, k_lat, preferred_element_type=f32)
            acc[d] = value if first else acc[d] * jnp.concatenate([alpha] * (LATENT // 128), axis=1) + value

    def spread(p):
        own = xall.at[0, 0, p]
        arrived(own, recv_d2.at[p] if p < 2 else recv_d3.at[p, 0])
        if p < 2:
            send(own, xall.at[0, 0, p + 2], send_d3.at[p + 2, 0], recv_d3.at[p + 2, 0], pair)
        for d in (2, 1, 3) if p < 2 else (1, 3):
            send(own, xall.at[NY - d, 0, p], send_d3.at[p, d], recv_d3.at[p, NY - d], at(z, yplus(d)))
        send(own, xall.at[0, 1, p], send_d3s.at[p, 0], recv_d3s.at[p, 0], (sec, sib))

    def share_rows(p):
        for d in (1, 3, 2):
            arrived(xall.at[d, 0, p], recv_d3.at[p, d])
            if d == 2 and p < 2:
                send(xall.at[2, 0, p], xall.at[2, 0, p + 2], send_d3.at[p + 2, 2], recv_d3.at[p + 2, 2], pair)
            send(xall.at[d, 0, p], xall.at[d, 1, p], send_d3s.at[p, d], recv_d3s.at[p, d], (sec, sib))

    n_rows = QUART * 8

    def experts(p):
        total = None
        for d in (0, 1, 3, 2):
            arrived(xall.at[d, 1, p], recv_d3s.at[p, d])
            rows = xall[d, :, p].astype(f32).reshape(2 * n_rows, COLS).astype(bf16)
            term = jnp.dot(rows, wgu[yplus(d)], preferred_element_type=f32)
            total = term if total is None else total + term
        gate, up = total[:, :128], total[:, 128:]
        active = (gate / (1.0 + jnp.exp(-gate)) * up).astype(bf16)
        for d in range(NY):
            piece = jnp.dot(active, wd[yplus(d)], preferred_element_type=f32).reshape(2, QUART, 8, COLS)
            own_sum[p, d] = piece[0]
            csib_send[p, d] = piece[1].astype(bf16)
        send(csib_send.at[p], csib_recv.at[p], send_c0.at[p], recv_c0.at[p], (sec, sib))

    def chunk(p, d):
        return own_sum[p, d] + csib_recv[p, d].astype(f32)

    def combine(p):
        arrived(csib_recv.at[p], recv_c0.at[p])
        if p >= 2:
            cy_send[p, 1] = chunk(p, 2).astype(bf16)
            send(cy_send.at[p, 1], pair_recv.at[0, p - 2], send_pair.at[0, p - 2], recv_pair.at[0, p - 2], pair)
        for d in (1, 3):
            cy_send[p, d - 1] = chunk(p, d).astype(bf16)
            send(
                cy_send.at[p, d - 1], cy_recv.at[p, NY - d - 1], send_c1.at[p, d], recv_c1.at[p, NY - d], at(z, yplus(d))
            )

    def combine_far(p):
        arrived(pair_recv.at[0, p], recv_pair.at[0, p])
        cy_send[p, 1] = (chunk(p, 2) + pair_recv[0, p].astype(f32)).astype(bf16)
        send(cy_send.at[p, 1], cy_recv.at[p, 1], send_c1.at[p, 2], recv_c1.at[p, 2], at(z, yplus(2)))

    def give_back(p):
        total = chunk(p, 0)
        for d in (1, 3, 2) if p < 2 else (1, 3):
            arrived(cy_recv.at[p, d - 1], recv_c1.at[p, d])
            total = total + cy_recv[p, d - 1].astype(f32)
        if p >= 2:
            csum[p] = total.astype(bf16)
            send(csum.at[p], pair_recv.at[1, p - 2], send_pair.at[1, p - 2], recv_pair.at[1, p - 2], pair)
            return
        arrived(pair_recv.at[1, p], recv_pair.at[1, p])
        csum[p] = (total + pair_recv[1, p].astype(f32)).astype(bf16)
        for k in reversed(range(QUART)):
            u = k + QUART * p
            home = ret.at[lax.div(z, 2)]
            if u == 0:
                pltpu.make_async_copy(csum.at[p, k], home, recv_c2).start()
            else:
                to = at(lax.rem(z + outward * u + NZ, NZ), y)
                send(csum.at[p, k], home, send_c2.at[p, k], recv_c2, to)

    def finish():
        arrived(ret, recv_c2)
        rows = ret[...].astype(f32).reshape(8 * EXPERTS, COLS).astype(bf16)
        weights = gates()
        high = weights.astype(bf16)
        low = (weights - high.astype(f32)).astype(bf16)
        mixture = jnp.dot(high, rows, preferred_element_type=f32) + jnp.dot(low, rows, preferred_element_type=f32)
        result = (hid[...] + mixture).reshape(NY, TOKENS, COLS)
        fin[...] = result.astype(bf16)
        for d in range(NY):
            to = (next_sec, (z * NY + yplus(d)) * 2 + c)
            send(fin.at[d], fin_recv.at[y], send_fin.at[d], recv_fin, to)

    def close(d):
        total = jnp.sum(l_ref[d], axis=1, keepdims=True)
        level = m_ref[d] * scale_log2 + jnp.log2(total)
        return level, acc[d] * (1.0 / total)

    def wide(factor):
        return jnp.concatenate([factor] * (LATENT // 128), axis=1)

    def column(ref, start, size):
        return jnp.transpose(jnp.broadcast_to(ref[0:1, start : start + size], (128, size)))

    half_rows = ROWS // 2

    def give_out_far():
        level, value = close(2)
        o_far[...] = value.astype(bf16).reshape(2, half_rows, LATENT)
        ls_far[...] = jnp.transpose(level)[:8, :]
        for q in range(2):
            to = at(z, yplus(1 + 2 * q))
            send(o_far.at[q], o_far_recv.at[q], send_o.at[q, 0], recv_o.at[q, 0], to)
            send(ls_far, ls_far_recv.at[q], send_o.at[q, 1], recv_o.at[q, 1], to)
        for q in range(2):
            to = at(z, yplus(1 + 2 * q))
            level, value = close(1 + 2 * q)
            m_ref[1 + 2 * q] = level
            acc[1 + 2 * q] = value
            rest = slice((1 - q) * half_rows, (2 - q) * half_rows)
            o_near[q, 1 - q] = value[rest].astype(bf16)
            send(o_near.at[q, 1 - q], o_recv.at[q, 1 - q], send_o.at[q, 2], recv_o.at[q, 2], to)

    def give_out_near():
        for q in range(2):
            to = at(z, yplus(1 + 2 * q))
            arrived(o_far_recv.at[q], recv_o.at[q, 0])
            arrived(ls_far_recv.at[q], recv_o.at[q, 1])
            rows = slice(q * half_rows, (q + 1) * half_rows)
            here, there = m_ref[1 + 2 * q, rows], column(ls_far_recv.at[q], q * half_rows, half_rows)
            best = jnp.maximum(here, there)
            here, there = jnp.exp2(here - best), jnp.exp2(there - best)
            norm = 1.0 / (here + there)
            value = acc[1 + 2 * q, rows] * wide(here * norm) + o_far_recv[q].astype(f32) * wide(there * norm)
            o_near[q, q] = value.astype(bf16)
            m_ref[1 + 2 * q, rows] = best + jnp.log2(here + there)
            ls_near[q] = jnp.transpose(m_ref[1 + 2 * q])[:8, :]
            send(o_near.at[q, q], o_recv.at[q, q], send_o.at[q, 3], recv_o.at[q, 3], to)
            send(ls_near.at[q], ls_recv.at[q], send_o.at[q, 4], recv_o.at[q, 4], to)

    def merge():
        level, value = close(0)
        levels, values = [level], [value]
        for q in range(2):
            arrived(o_recv.at[q, 1 - q], recv_o.at[q, 2])
            arrived(o_recv.at[q, q], recv_o.at[q, 3])
            arrived(ls_recv.at[q], recv_o.at[q, 4])
            levels.append(column(ls_recv.at[q], 0, ROWS))
            values.append(o_recv[q].reshape(ROWS, LATENT).astype(f32))
        best = functools.reduce(jnp.maximum, levels)
        shares = [jnp.exp2(one - best) for one in levels]
        norm = 1.0 / functools.reduce(jnp.add, shares)
        out_ref[...] = sum(one * wide(share * norm) for one, share in zip(values, shares)).astype(bf16)

    def queries_on():
        for d in (1, 3):
            q = d // 2
            rows = pl.ds(q * half_rows, half_rows)
            to = at(z, yplus(NY - d))
            arrived(ql.at[d], recv_q.at[0, d])
            send(ql.at[d, rows], ql.at[2, rows], send_q.at[2, q], recv_q.at[2, q], to)
            arrived(qraw.at[d], recv_q.at[1, d])
            if q == 0:
                send(qraw.at[d], qraw.at[2], send_q.at[1, 2], recv_q.at[1, 2], to)

    def queries():
        for q in range(2):
            arrived(ql.at[2, pl.ds(q * half_rows, half_rows)], recv_q.at[2, q])
        arrived(qraw.at[2], recv_q.at[1, 2])
        locals_[0].wait()
        spread_rope()

    def weights_here():
        for copy in locals_[1:]:
            copy.wait()

    dispatch()
    ring(0)
    qraw[0] = qrope_ref[...]
    ring(1)
    spread(0)
    queries_on()
    ring(2)
    spread(2)
    spread(1)
    ring(3)
    share_rows(0)
    spread(3)
    share_rows(2)
    ring(4)
    keep_rows()
    weights_here()
    experts(0)
    share_rows(1)
    experts(2)
    ring(5)
    share_rows(3)
    combine(2)
    experts(1)
    combine(0)
    experts(3)
    ring(6)
    combine(3)
    combine(1)
    combine_far(0)
    queries()
    give_back(2)
    attend(1, True)
    ring(7)
    attend(2, False)
    combine_far(1)
    attend(3, False)
    give_back(3)
    attend(4, False)
    ring(8)
    attend(5, False)
    give_back(0)
    attend(6, False)
    attend(7, False)
    give_back(1)
    attend(0, False)
    give_out_far()
    give_out_near()
    finish()
    merge()
    arrived(fin_recv, recv_fin)
    for k in range(NY):
        passed_ref[:, k * COLS : (k + 1) * COLS] = fin_recv[k]
    for copy in sends:
        copy.wait_send()


def per_device(
    hidden_rows, expert_ids, gate_weights, w_gate, w_up, w_down, query_latent, query_rope, cache_latent, cache_rope, offsets
):
    vmem = pl.BlockSpec(memory_space=pltpu.VMEM)
    anywhere = pl.BlockSpec(memory_space=pl.ANY)
    dma = pltpu.SemaphoreType.DMA
    passed, attended = pl.pallas_call(
        kernel,
        out_shape=(
            jax.ShapeDtypeStruct((TOKENS, WIDTH), bf16),
            jax.ShapeDtypeStruct((ROWS, LATENT), bf16),
        ),
        in_specs=[
            anywhere, anywhere, anywhere, anywhere, anywhere, anywhere, anywhere, anywhere, anywhere, anywhere,
            pl.BlockSpec(memory_space=pltpu.SMEM),
        ],
        out_specs=(vmem, vmem),
        scratch_shapes=[
            pltpu.VMEM((HALF, 4, KEYS, KW), bf16),
            pltpu.VMEM((NY, ROWS, LATENT), bf16),
            pltpu.VMEM((NY, TOKENS, HEADS * ROPE), bf16),
            pltpu.VMEM((NY, ROWS, 128), bf16),
            pltpu.VMEM((ROWS, 128), f32),
            pltpu.VMEM((NY, ROWS, LATENT), f32),
            pltpu.VMEM((NY, ROWS, 128), f32),
            pltpu.VMEM((NY, ROWS, 128), f32),
            pltpu.VMEM((2, ROWS // 2, LATENT), bf16),
            pltpu.VMEM((2, ROWS // 2, LATENT), bf16),
            pltpu.VMEM((2, 2, ROWS // 2, LATENT), bf16),
            pltpu.VMEM((2, 2, ROWS // 2, LATENT), bf16),
            pltpu.VMEM((8, ROWS), f32),
            pltpu.VMEM((2, 8, ROWS), f32),
            pltpu.VMEM((2, 8, ROWS), f32),
            pltpu.VMEM((2, 8, ROWS), f32),
            pltpu.VMEM((NY, 2 * EXPERTS, COLS), bf16),
            pltpu.VMEM((NY, 2 * EXPERTS, COLS), bf16),
            pltpu.VMEM((NY, TOKENS, 128), f32),
            pltpu.VMEM((EXPERTS, 8, COLS), bf16),
            pltpu.VMEM((NY * TOKENS, COLS), f32),
            pltpu.VMEM((NY, 2, PARTS, QUART, 8, COLS), bf16),
            pltpu.VMEM((NY, COLS, 256), bf16),
            pltpu.VMEM((NY, 128, COLS), bf16),
            pltpu.VMEM((PARTS, NY, QUART, 8, COLS), bf16),
            pltpu.VMEM((PARTS, NY, QUART, 8, COLS), bf16),
            pltpu.VMEM((PARTS, NY, QUART, 8, COLS), f32),
            pltpu.VMEM((PARTS, NY - 1, QUART, 8, COLS), bf16),
            pltpu.VMEM((PARTS, NY - 1, QUART, 8, COLS), bf16),
            pltpu.VMEM((PARTS, QUART, 8, COLS), bf16),
            pltpu.VMEM((2, 2, QUART, 8, COLS), bf16),
            pltpu.VMEM((EXPERTS, 8, COLS), bf16),
            pltpu.VMEM((NY, TOKENS, COLS), bf16),
            pltpu.VMEM((NY, TOKENS, COLS), bf16),
            dma((HALF, 2)), dma((HALF, 2)),
            dma((HALF, 2)), dma((HALF, 2)),
            dma((3, NY)), dma((3, NY)),
            dma((2, 5)), dma((2, 5)),
            dma((2, NY)), dma((2,)),
            dma((HALF,)), dma((2,)),
            dma((PARTS, NY)), dma((PARTS, NY)),
            dma((PARTS, NY)), dma((PARTS, NY)),
            dma((PARTS,)), dma((PARTS,)),
            dma((PARTS, NY)), dma((PARTS, NY)),
            dma((2, 2)), dma((2, 2)),
            dma((2, QUART)), dma,
            dma((NY,)), dma,
            dma((NY, 3)), dma((1,)),
            pltpu.VMEM((TOKENS, WIDTH), bf16),
            pltpu.VMEM((2, TOKENS), jnp.int32),
            pltpu.VMEM((2, TOKENS), f32),
            pltpu.VMEM((TOKENS, HEADS * ROPE), bf16),
            pltpu.VMEM((KEYS, LATENT), bf16),
            pltpu.VMEM((KEYS, ROPE), bf16),
            dma((6,)),
        ],
        compiler_params=pltpu.CompilerParams(
            collective_id=0, has_side_effects=True, vmem_limit_bytes=56 * 1024 * 1024
        ),
        cost_estimate=pl.CostEstimate(flops=6_000_000_000, bytes_accessed=4_000_000, transcendentals=2_000_000),
        name="layer",
    )(
        hidden_rows[0], expert_ids[0].T, gate_weights[0].T, w_gate[0], w_up[0], w_down[0],
        query_latent.reshape(ROWS, LATENT), query_rope[0], cache_latent[0], cache_rope[0], offsets,
    )
    return passed[None], attended.reshape(1, TOKENS, HEADS, LATENT)


def solution(mesh):
    rows = P("section", "expert", None)
    heads = P("section", "expert", None, None)
    return jax.shard_map(
        per_device,
        mesh=mesh,
        in_specs=(rows, rows, rows, P("section", None, "expert"), P("section", None, "expert"), rows, heads, rows, rows, rows, P("section")),
        out_specs=(rows, heads),
        check_vma=False,
    )
```
